512 devices in a mesh: req: 32 (over z, x), prefix: 16 (over y, core).
Axes of the slice: x: 4, y: 8, z: 8, core: 2. Of those that a mesh axis runs over, the one named last changes fastest.
Arguments:
- queries: bfloat16 [2, 1024, 8192], P(None, ('req', 'prefix')), may hold values from -20 to 20
- prefix_keys: bfloat16 [6144, 1024], P('prefix'), may hold values from -6.25 to 6.25
- prefix_values: bfloat16 [6144, 1024], P('prefix'), may hold values from -6 to 6
- pool_keys: bfloat16 [1024, 128, 1024], P(('req', 'prefix')), may hold values from -8 to 8
- pool_values: bfloat16 [1024, 128, 1024], P(('req', 'prefix')), may hold values from -6 to 6
- new_keys: bfloat16 [2, 1024, 1024], P(None, ('req', 'prefix')), may hold values from -10 to 10
- new_values: bfloat16 [2, 1024, 1024], P(None, ('req', 'prefix')), may hold values from -6 to 6
- block_table: int32 [1024, 16], replicated, may hold values from 0 to 63, as said below
- suffix_lengths: int32 [1024], replicated, may hold values from 0 to 2048, as said below
Outputs:
- attended: bfloat16 [2, 1024, 8192], P(None, ('req', 'prefix'))
The draws below stay inside these ranges and needn't reach their ends.
Inputs may be any that keep to these rules, and one draw needn't show every extreme that they name: `block_table`: requests 2 g * 32 to (2 g + 2) * 32 - 1 form pair g, whose pool is pool rows 2 g * 16 * 2 onward, 64 of them. Entry j of request i, for j * 128 < suffix_lengths[i], is the slot in the pair's pool that holds that block; every slot of a pair's pool holds exactly one live block; other entries are arbitrary slot numbers. `suffix_lengths`: in each pair one request has 2048 suffix positions, 48 requests have 1 to 128, and the rest none.
All inputs are finite; a program needn't handle non-finite values.
Results may differ from the reference program's by a relative error of at most 0.0023.
Values may be sent and summed in bfloat16 or wider, within the bound.
No kernel may reach another device: no remote copies, remote signals or barrier semaphores. Data moves between devices by JAX's collectives and lax.ppermute only.
A program may use at most 128 MiB of HBM per device.

```python
import math
import jax
import jax.numpy as jnp
from jax import lax

H = 64
KVH = 8
DH = 128
BLK = 128
MAXB = 16
SLOTS = 2
REQ_DEV = 32
REQS = 1024
PRE = 6144
POOL = 1024
N_REQ = 32
N_PREFIX = 16


def allocation(key):
    pair_rows = 2 * REQ_DEV
    pair_pool = 2 * N_PREFIX * SLOTS
    base_key = jax.random.fold_in(key, 2000)

    def one_pair(pair):
        sub_key = jax.random.fold_in(base_key, pair)
        order = jax.random.permutation(jax.random.fold_in(sub_key, 1), pair_rows)
        slot_order = jax.random.permutation(jax.random.fold_in(sub_key, 2), pair_pool)
        rank = jnp.zeros((pair_rows,), jnp.int32).at[order].set(jnp.arange(pair_rows, dtype=jnp.int32))
        spare = jax.random.randint(jax.random.fold_in(sub_key, 3), (pair_rows, MAXB), 0, pair_pool)
        big_row = slot_order[:MAXB]
        single = slot_order[jnp.clip(MAXB + rank - 1, 0, pair_pool - 1)]
        column = jnp.arange(MAXB)
        is_single = (rank >= 1) & (rank <= pair_pool - MAXB)
        pair_table = jnp.where(rank[:, None] == 0, big_row[None, :], jnp.where(is_single[:, None] & (column[None, :] == 0), single[:, None], spare))
        short_len = jax.random.randint(jax.random.fold_in(sub_key, 4), (pair_rows,), 1, BLK + 1)
        lengths = jnp.where(rank == 0, MAXB * BLK, jnp.where(is_single, short_len, 0))
        return (pair_table, lengths)
    tables, lengths = jax.vmap(one_pair)(jnp.arange(N_REQ // 2))
    return (tables.reshape(REQS, MAXB).astype(jnp.int32), lengths.reshape(REQS).astype(jnp.int32))


def draw_block_table(key, part):
    return allocation(key)[0]


def draw_suffix_lengths(key, part):
    return allocation(key)[1]


def draw_queries(key, part):
    key = jax.random.fold_in(key, 1001)
    return (5.0 * jnp.clip(jax.random.normal(key, (2, REQS, H * DH), jnp.float32), -4.0, 4.0)).astype(jnp.bfloat16)


def draw_prefix_keys(key, part):
    key = jax.random.fold_in(key, 1002)
    return jnp.clip(jax.random.normal(key, (PRE, KVH * DH), jnp.float32), -4.0, 4.0).astype(jnp.bfloat16)


def block_scale(rng, shape, split, smallest, largest):
    loudness, own = 1.0, jax.random.fold_in(rng, 6)
    for dim, blocks in split:
        draws = jnp.exp(jax.random.uniform(jax.random.fold_in(own, dim), (blocks,), jnp.float32, smallest / len(split), largest / len(split)))
        loudness = loudness * jnp.repeat(draws, shape[dim] // blocks).reshape([-1 if axis == dim else 1 for axis in range(len(shape))])
    return loudness


def gaussian(key, dims, scale, limit, shards=(), kind=jnp.bfloat16):
    drawn = jax.random.normal(key, dims, jnp.float32) * scale
    if len(shards) > 0:
        drawn = block_scale(key, dims, shards, -0.22, 0.18) * drawn
    return jnp.clip(drawn, min=-limit, max=limit).astype(kind)


def setup_inputs(seed: int = 0) -> dict:
    key_list = jax.random.split(jax.random.key(seed), 10)
    queries = draw_queries(jax.random.fold_in(key_list[9], 71), 0)
    prefix_keys = draw_prefix_keys(jax.random.fold_in(key_list[9], 71), 0)
    prefix_values = gaussian(key_list[2], (PRE, KVH * DH), 1.0, 6.0, ((0, 16),))
    pool_keys = gaussian(key_list[3], (POOL, BLK, KVH * DH), 1.4, 8.0, ((0, 512),))
    pool_values = gaussian(key_list[4], (POOL, BLK, KVH * DH), 1.0, 6.0, ((0, 512),))
    new_keys = gaussian(key_list[5], (2, REQS, KVH * DH), 1.8, 10.0, ((1, 512),))
    new_values = gaussian(key_list[6], (2, REQS, KVH * DH), 1.0, 6.0, ((1, 512),))
    block_table = draw_block_table(jax.random.fold_in(key_list[9], 71), 0)
    suffix_lengths = draw_suffix_lengths(jax.random.fold_in(key_list[9], 71), 0)
    return {"queries": queries, "prefix_keys": prefix_keys, "prefix_values": prefix_values, "pool_keys": pool_keys, "pool_values": pool_values, "new_keys": new_keys, "new_values": new_values, "block_table": block_table, "suffix_lengths": suffix_lengths}


NEG = -1e+30

def block_terms(scores, live):
    masked = jnp.where(live, scores, NEG)
    block_peak = lax.optimization_barrier(jnp.max(masked, axis=-1))
    weights = jnp.where(live, jnp.exp(masked - block_peak[..., None]), 0.0).astype(jnp.bfloat16)
    weights = lax.optimization_barrier(weights).astype(jnp.float32)
    block_total = lax.optimization_barrier(jnp.sum(weights, axis=-1))
    return (block_peak, weights, block_total)

def reference(queries, prefix_keys, prefix_values, pool_keys, pool_values, new_keys, new_values, block_table, suffix_lengths):
    group_size = H // KVH
    scaling = 1.0 / math.sqrt(DH)
    batch_rows = 16
    pair_rows = 2 * REQ_DEV
    pair_pool = 2 * N_PREFIX * SLOTS
    request_ids = jnp.arange(REQS, dtype=jnp.int32)
    pool_rows = (block_table + (request_ids // pair_rows * pair_pool)[:, None]).astype(jnp.int32)
    prefix_k = prefix_keys.astype(jnp.float32).reshape(PRE // BLK, BLK, KVH, DH)
    prefix_v = prefix_values.astype(jnp.float32).reshape(PRE // BLK, BLK, KVH, DH)
    new_live = (jnp.arange(2)[None, :] <= jnp.arange(2)[:, None])[:, None, None, None, :]
    places = jnp.arange(MAXB, dtype=jnp.int32)[:, None] * BLK + jnp.arange(BLK, dtype=jnp.int32)[None, :]

    def one_batch(start):
        query_tiles = lax.dynamic_slice_in_dim(queries, start, batch_rows, 1).astype(jnp.float32)
        query_tiles = query_tiles.reshape(2, batch_rows, KVH, group_size, DH)
        scores = jnp.einsum('srkgd,nbkd->srkgnb', query_tiles, prefix_k) * scaling
        pre_peak, pre_weights, pre_total = block_terms(scores, True)
        pre_out = jnp.einsum('srkgnb,nbkd->srkgnd', pre_weights, prefix_v)
        rows_here = lax.dynamic_slice_in_dim(pool_rows, start, batch_rows, 0)
        lengths = lax.dynamic_slice_in_dim(suffix_lengths, start, batch_rows, 0)
        suffix_k = pool_keys[rows_here].astype(jnp.float32).reshape(batch_rows, MAXB, BLK, KVH, DH)
        suffix_v = pool_values[rows_here].astype(jnp.float32).reshape(batch_rows, MAXB, BLK, KVH, DH)
        live = (places[None] < lengths[:, None, None])[None, :, None, None]
        scores = jnp.einsum('srkgd,rnbkd->srkgnb', query_tiles, suffix_k) * scaling
        suf_peak, suf_weights, suf_total = block_terms(scores, live)
        suf_out = jnp.einsum('srkgnb,rnbkd->srkgnd', suf_weights, suffix_v)
        fresh_k = lax.dynamic_slice_in_dim(new_keys, start, batch_rows, 1).astype(jnp.float32).reshape(2, batch_rows, KVH, DH)
        fresh_v = lax.dynamic_slice_in_dim(new_values, start, batch_rows, 1).astype(jnp.float32).reshape(2, batch_rows, KVH, DH)
        scores = jnp.einsum('srkgd,nrkd->srkgn', query_tiles, fresh_k) * scaling
        new_peak, new_weights, new_total = block_terms(scores, new_live)
        new_out = jnp.einsum('srkgn,nrkd->srkgd', new_weights, fresh_v)
        all_peak = jnp.concatenate([pre_peak, suf_peak, new_peak[..., None]], axis=4)
        all_out = jnp.concatenate([pre_out, suf_out, new_out[..., None, :]], axis=4)
        all_total = jnp.concatenate([pre_total, suf_total, new_total[..., None]], axis=4)
        row_top = lax.optimization_barrier(jnp.max(all_peak, axis=4, keepdims=True))
        factor = jnp.exp(all_peak - row_top)
        numer = lax.optimization_barrier(jnp.sum(factor[..., None] * all_out, axis=4))
        denom = lax.optimization_barrier(jnp.sum(factor * all_total, axis=4))
        return (numer / denom[..., None]).astype(jnp.bfloat16).reshape(2, batch_rows, H * DH)
    starts = jnp.arange(REQS // batch_rows, dtype=jnp.int32) * batch_rows
    batches = lax.map(one_batch, starts)
    return jnp.transpose(batches, (1, 0, 2, 3)).reshape(2, REQS, H * DH)
```

```python
import functools
import math

import jax
import jax.numpy as jnp
from jax import lax
from jax.experimental import pallas as pl
from jax.experimental.pallas import tpu as pltpu
from jax.sharding import PartitionSpec as P

H = 64
KVH = 8
DH = 128
BLK = 128
GROUP = H // KVH
HALF = KVH // 2
NEG = -1e30
LOG2E = 1.0 / math.log(2.0)
EXPO = LOG2E / math.sqrt(DH)
LIFT = 8192.0

bf16 = jnp.bfloat16
f32 = jnp.float32
NT = (((1,), (1,)), ((), ()))
VM = pl.BlockSpec(memory_space=pltpu.VMEM)
SM = pl.BlockSpec(memory_space=pltpu.SMEM)
ANY = pl.BlockSpec(memory_space=pl.ANY)


def prepare_kernel(q_ref, nk_ref, nv_ref, len_ref, table_ref, qt_ref, nkp_ref, nvp_ref, meta_ref, rows_ref, sem):
    req = lax.axis_index("req")
    pre = lax.axis_index("prefix")
    pair_rows = rows_ref.shape[0]
    n_pre = pair_rows // 4
    pair = req // 2
    side = req % 2
    copy = pltpu.make_async_copy(
        table_ref.at[pl.ds(pl.multiple_of(pair * pair_rows, pair_rows), pair_rows), :], rows_ref, sem
    )
    copy.start()
    pieces = []
    steps = [q_ref[s].astype(f32) for s in range(2)]
    for head in range(H):
        for s in range(2):
            pieces.append(steps[s][:, head * DH : (head + 1) * DH])
    qt_ref[...] = jnp.concatenate(pieces, axis=0).astype(bf16)
    for src, dst in ((nk_ref, nkp_ref), (nv_ref, nvp_ref)):
        top = jnp.concatenate([src[0].astype(f32), src[1].astype(f32), jnp.zeros((12, KVH * DH), f32)], axis=0)
        dst[...] = jnp.zeros(dst.shape, bf16)
        dst[0:16, :] = top.astype(bf16)
    lane = lax.broadcasted_iota(jnp.int32, (pair_rows, 128), 1)
    row = lax.broadcasted_iota(jnp.int32, (pair_rows, 128), 0)
    per_line = 128 // pair_rows
    line = len_ref[pl.ds(pair // per_line, 1), :]
    at = row + (pair % per_line) * pair_rows
    lengths = jnp.sum(jnp.where(lane == at, jnp.broadcast_to(line, (pair_rows, 128)), 0), axis=1, keepdims=True)
    copy.wait()
    blocks = rows_ref.shape[1]
    table = rows_ref[...]
    col = lax.broadcasted_iota(jnp.int32, (pair_rows, blocks), 1)
    trow = lax.broadcasted_iota(jnp.int32, (pair_rows, blocks), 0)
    left = jnp.broadcast_to(lengths, (pair_rows, blocks)) - col * BLK
    for n in range(4):
        holder = side if n < 2 else 1 - side
        slot = (holder * n_pre + pre) * 2 + n % 2
        hit = (table == slot) & (left > 0)
        owner = jnp.sum(jnp.where(hit, trow, 0)) - side * (pair_rows // 2)
        live = jnp.sum(jnp.where(hit, jnp.minimum(left, BLK), 0))
        mine = (owner >= 0) & (owner < pair_rows // 2)
        owner = jnp.where(mine, owner, 0)
        meta_ref[n, 0] = owner // 2
        meta_ref[n, 1] = owner % 2
        meta_ref[n, 2] = jnp.where(mine, live, 0)


def attend_kernel(
    flip, q_ref, pk_ref, pv_ref, ok_ref, ov_ref, xk_ref, xv_ref, nk_ref, nv_ref, meta_ref,
    out_ref, m_s, t_s, a_s, l_s,
):
    pre = lax.axis_index("prefix")
    half = pre % 2
    if flip:
        half = 1 - half
    n_dev = q_ref.shape[0]
    rows = n_dev * 32
    ones = jnp.ones((BLK, DH), bf16)
    lane = lax.broadcasted_iota(jnp.int32, (32, BLK), 1)
    row = lax.broadcasted_iota(jnp.int32, (32, BLK), 0)
    row_req = row % 2
    row_step = row // 2 % 2
    new_live = (lane < 4) & (lane % 2 == row_req) & (lane // 2 <= row_step)
    n_blocks = pk_ref.shape[0] // BLK
    for i in range(HALF):
        kvh = half * HALF + i
        lanes = pl.ds(pl.multiple_of(kvh * DH, DH), DH)
        qrows = pl.ds(pl.multiple_of(kvh * 32, 32), 32)
        q = q_ref[:, qrows, :].reshape(rows, DH)
        peaks, outs = [], []
        for b in range(n_blocks):
            span = slice(b * BLK, (b + 1) * BLK)
            s = lax.dot_general(q, pk_ref[span, lanes], NT, preferred_element_type=f32)
            peak = jnp.max(s, axis=1, keepdims=True)
            w = jnp.exp2((s - peak) * EXPO).astype(bf16)
            v = jnp.concatenate([pv_ref[span, lanes], ones], axis=1)
            peaks.append(peak)
            outs.append(jnp.dot(w, v, preferred_element_type=f32))
        top = functools.reduce(jnp.maximum, peaks)
        both = 0.0
        for peak, o in zip(peaks, outs):
            both = both + jnp.exp2((peak - top) * EXPO) * o
        m_s[...] = jnp.broadcast_to(top, (rows, DH)).reshape(n_dev, 32, DH)
        a_s[...] = both[:, :DH].reshape(n_dev, 32, DH)
        t_s[...] = both[:, DH:].reshape(n_dev, 32, DH)
        extra = []
        for n in range(5):
            if n < 4:
                kr, vr = (ok_ref, ov_ref) if n < 2 else (xk_ref, xv_ref)
                dev = meta_ref[n, 0]
                k, v = kr[n % 2, :, lanes], vr[n % 2, :, lanes]
                live = (row_req == meta_ref[n, 1]) & (lane < meta_ref[n, 2])
            else:
                dev = pre
                k, v = nk_ref[:, lanes], nv_ref[:, lanes]
                live = new_live
            s = lax.dot_general(q_ref[dev, qrows, :], k, NT, preferred_element_type=f32)
            s = jnp.where(live, s, NEG)
            peak = jnp.max(s, axis=1, keepdims=True)
            w = jnp.where(live, jnp.exp2((s - peak) * EXPO), 0.0).astype(bf16)
            o = jnp.dot(w, jnp.concatenate([v, ones], axis=1), preferred_element_type=f32)
            extra.append((dev, peak, o))
        for dev, peak, o in extra:
            old = m_s[dev]
            new = jnp.maximum(old, peak)
            fa = jnp.exp2((old - new) * EXPO)
            fb = jnp.exp2((peak - new) * EXPO)
            m_s[dev] = new
            a_s[dev] = a_s[dev] * fa + o[:, :DH] * fb
            t_s[dev] = t_s[dev] * fa + o[:, DH:] * fb
        total = t_s[...]
        out_ref[:, i * 32 : (i + 1) * 32, :] = a_s[...] / total
        l_s[:, i * 32 : (i + 1) * 32, :] = m_s[...] * EXPO + jnp.log(total) * LOG2E
    eye = lax.broadcasted_iota(jnp.int32, (DH, DH), 0) == lax.broadcasted_iota(jnp.int32, (DH, DH), 1)
    for dev in range(n_dev):
        line = jnp.sum(jnp.where(eye, l_s[dev], 0.0), axis=0, keepdims=True)
        out_ref[dev, 128:136, :] = jnp.broadcast_to(line, (8, DH))


def columns(lines):
    pad = jnp.zeros((DH - lines.shape[0], DH), f32)
    return jnp.concatenate([lines, pad], axis=0).T


def core_merge_kernel(a_ref, b_ref, out_ref):
    n_dev = a_ref.shape[0]
    la = a_ref[:, 128:136, :][:, 0, :]
    lb = b_ref[:, 128:136, :][:, 0, :]
    top = jnp.maximum(la, lb)
    wa = jnp.exp2(la - top)
    wb = jnp.exp2(lb - top)
    total = wa + wb
    lse = top + jnp.log(total) * LOG2E
    hi = lse.astype(bf16).astype(f32)
    mid = (lse - hi).astype(bf16).astype(f32)
    low = lse - hi - mid
    ca = columns(wa * (LIFT / total))
    cb = columns(wb * (LIFT / total))
    for dev in range(n_dev):
        out_ref[dev, 0:128, :] = (
            a_ref[dev, 0:128, :] * ca[:, dev : dev + 1] + b_ref[dev, 0:128, :] * cb[:, dev : dev + 1]
        )
        out_ref[dev, 128:136, :] = jnp.concatenate(
            [hi[dev : dev + 1], mid[dev : dev + 1], low[dev : dev + 1], jnp.zeros((5, DH), f32)], axis=0
        )


def final_kernel(z_ref, out_ref):
    n_dev = z_ref.shape[0]
    for c in range(2):
        lines = []
        for src in range(c, n_dev, 2):
            parts = z_ref[src, 128:136, :]
            lines.append(jnp.sum(parts, axis=0, keepdims=True))
        lse = jnp.concatenate(lines, axis=0)
        w = jnp.exp2(lse - jnp.max(lse, axis=0, keepdims=True))
        w = columns(w / (LIFT * jnp.sum(w, axis=0, keepdims=True)))
        o = 0.0
        for y, src in enumerate(range(c, n_dev, 2)):
            o = o + z_ref[src, 0:128, :] * w[:, y : y + 1]
        for h in range(H // 2):
            head = c * (H // 2) + h
            for s in range(2):
                r = h * 4 + s * 2
                out_ref[s, :, head * DH : (head + 1) * DH] = o[r : r + 2, :].astype(bf16)


def call(kernel, out_shape, ins, out_specs=VM, scratch=(), flops=0, moved=0, name=None):
    return pl.pallas_call(
        kernel,
        out_shape=out_shape,
        in_specs=ins,
        out_specs=out_specs,
        scratch_shapes=list(scratch),
        compiler_params=pltpu.CompilerParams(vmem_limit_bytes=40 * 1024 * 1024),
        cost_estimate=pl.CostEstimate(flops=flops, bytes_accessed=moved, transcendentals=0),
        name=name,
    )


def per_device(
    queries,
    prefix_keys,
    prefix_values,
    pool_keys,
    pool_values,
    new_keys,
    new_values,
    block_table,
    suffix_lengths,
):
    n_req = lax.axis_size("req")
    n_pre = lax.axis_size("prefix")
    pair_rows = 4 * n_pre
    swap = [(i, i ^ 1) for i in range(n_req)]
    core = [(i, i ^ 1) for i in range(n_pre)]
    far_keys = lax.ppermute(pool_keys, "req", swap)
    far_values = lax.ppermute(pool_values, "req", swap)
    sds = jax.ShapeDtypeStruct
    own, nk, nv, meta = call(
        prepare_kernel,
        (sds((4 * H, DH), bf16), sds((BLK, KVH * DH), bf16), sds((BLK, KVH * DH), bf16), sds((4, 3), jnp.int32)),
        [VM, VM, VM, VM, ANY],
        (VM, VM, VM, SM),
        [pltpu.VMEM((pair_rows, block_table.shape[1]), jnp.int32), pltpu.SemaphoreType.DMA],
        name="prepare",
    )(queries, new_keys, new_values, suffix_lengths.reshape(-1, 128), block_table)
    group = lax.all_gather(own, "prefix", axis=0)
    partial = sds((n_pre, 136, DH), f32)
    state = pltpu.VMEM((n_pre, 32, DH), f32)

    def attend(flip):
        return call(
            functools.partial(attend_kernel, flip),
            partial,
            [VM] * 9 + [SM],
            VM,
            [state, state, state, pltpu.VMEM((n_pre, 128, DH), f32)],
            flops=800_000_000,
            moved=6_000_000,
            name="attend_other" if flip else "attend_own",
        )(group, prefix_keys, prefix_values, pool_keys, pool_values, far_keys, far_values, nk, nv, meta)

    theirs = lax.ppermute(attend(True), "prefix", core)
    mine = attend(False)
    merged = call(core_merge_kernel, partial, [VM, VM], moved=4_000_000, name="core_merge")(mine, theirs)
    spread = lax.all_to_all(merged.astype(jnp.float16), "prefix", 0, 0, tiled=True)
    return call(final_kernel, sds((2, 2, H * DH), bf16), [VM], moved=1_000_000, name="final")(
        spread.astype(f32)
    )


def solution(mesh):
    placed = (
        P(None, ("req", "prefix"), None),
        P("prefix", None),
        P("prefix", None),
        P(("req", "prefix"), None, None),
        P(("req", "prefix"), None, None),
        P(None, ("req", "prefix"), None),
        P(None, ("req", "prefix"), None),
        P(),
        P(),
    )
    return jax.shard_map(
        per_device,
        mesh=mesh,
        in_specs=placed,
        out_specs=P(None, ("req", "prefix"), None),
        check_vma=False,
    )
```

```python
import functools
import math

import jax
import jax.numpy as jnp
from jax import lax
from jax.experimental import pallas as pl
from jax.experimental.pallas import tpu as pltpu
from jax.sharding import PartitionSpec as P

H = 64
KVH = 8
DH = 128
BLK = 128
GROUP = H // KVH
HALF = KVH // 2
NEG = -1e30
LOG2E = 1.0 / math.log(2.0)
EXPO = LOG2E / math.sqrt(DH)
LIFT = 8192.0
QLIFT = 2048.0

bf16 = jnp.bfloat16
f32 = jnp.float32
NT = (((1,), (1,)), ((), ()))
VM = pl.BlockSpec(memory_space=pltpu.VMEM)
SM = pl.BlockSpec(memory_space=pltpu.SMEM)
ANY = pl.BlockSpec(memory_space=pl.ANY)


def prepare_kernel(
    q_ref, nk_ref, nv_ref, len_ref, table_ref, qt_ref, nkp_ref, nvp_ref, meta_ref,
    q_s, nk_s, nv_s, len_s, table_s, sems,
):
    req = lax.axis_index("req")
    pre = lax.axis_index("prefix")
    n_pre = lax.axis_size("prefix")
    pair_rows = 4 * n_pre
    per_line = 128 // pair_rows
    pair = req // 2
    side = req % 2
    line = pair // per_line
    first = (pair % per_line) * pair_rows
    lanes = pl.ds(pl.multiple_of(line * 128, 128), 128)
    sources = (len_ref, table_ref.at[:, lanes], q_ref, nk_ref, nv_ref)
    copies = [
        pltpu.make_async_copy(src, dst, sems.at[i])
        for i, (src, dst) in enumerate(zip(sources, (len_s, table_s, q_s, nk_s, nv_s)))
    ]
    for copy in copies:
        copy.start()
    for copy in copies:
        copy.wait()
    pieces = []
    steps = [q_s[s].astype(f32) * QLIFT for s in range(2)]
    for head in range(H):
        for s in range(2):
            pieces.append(steps[s][:, head * DH : (head + 1) * DH])
    qt_ref[...] = jnp.concatenate(pieces, axis=0)
    for src, dst in ((nk_s, nkp_ref), (nv_s, nvp_ref)):
        top = jnp.concatenate([src[0].astype(f32), src[1].astype(f32), jnp.zeros((12, KVH * DH), f32)], axis=0)
        dst[...] = jnp.zeros(dst.shape, bf16)
        dst[0:16, :] = top.astype(bf16)
    table = table_s[...]
    lane = lax.broadcasted_iota(jnp.int32, table.shape, 1) - first
    block = lax.broadcasted_iota(jnp.int32, table.shape, 0)
    left = jnp.broadcast_to(len_s[pl.ds(line, 1), :], table.shape) - block * BLK
    usable = (left > 0) & (lane >= 0) & (lane < pair_rows)
    for n in range(4):
        holder = side if n < 2 else 1 - side
        slot = (holder * n_pre + pre) * 2 + n % 2
        hit = (table == slot) & usable
        owner = jnp.sum(jnp.where(hit, lane, 0)) - side * (pair_rows // 2)
        live = jnp.sum(jnp.where(hit, jnp.minimum(left, BLK), 0))
        mine = (owner >= 0) & (owner < pair_rows // 2)
        owner = jnp.where(mine, owner, 0)
        meta_ref[n, 0] = owner // 2
        meta_ref[n, 1] = owner % 2
        meta_ref[n, 2] = jnp.where(mine, live, 0)


def attend_kernel(
    flip, q_ref, pk_ref, pv_ref, ok_ref, ov_ref, xk_ref, xv_ref, nk_ref, nv_ref, meta_ref,
    out_ref, m_s, t_s, a_s, l_s,
):
    pre = lax.axis_index("prefix")
    half = pre % 2
    if flip:
        half = 1 - half
    n_dev = q_ref.shape[0]
    rows = n_dev * 32
    ones = jnp.ones((BLK, DH), bf16)
    lane = lax.broadcasted_iota(jnp.int32, (32, BLK), 1)
    row = lax.broadcasted_iota(jnp.int32, (32, BLK), 0)
    row_req = row % 2
    row_step = row // 2 % 2
    new_live = (lane < 4) & (lane % 2 == row_req) & (lane // 2 <= row_step)
    n_blocks = pk_ref.shape[0] // BLK
    for i in range(HALF):
        kvh = half * HALF + i
        lanes = pl.ds(pl.multiple_of(kvh * DH, DH), DH)
        qrows = pl.ds(pl.multiple_of(kvh * 32, 32), 32)
        q = q_ref[:, qrows, :].reshape(rows, DH)
        peaks, outs = [], []
        for b in range(n_blocks):
            span = slice(b * BLK, (b + 1) * BLK)
            s = lax.dot_general(q, pk_ref[span, lanes], NT, preferred_element_type=f32)
            peak = jnp.max(s, axis=1, keepdims=True)
            w = jnp.exp2((s - peak) * EXPO).astype(bf16)
            v = jnp.concatenate([pv_ref[span, lanes], ones], axis=1)
            peaks.append(peak)
            outs.append(jnp.dot(w, v, preferred_element_type=f32))
        top = functools.reduce(jnp.maximum, peaks)
        both = 0.0
        for peak, o in zip(peaks, outs):
            both = both + jnp.exp2((peak - top) * EXPO) * o
        m_s[...] = jnp.broadcast_to(top, (rows, DH)).reshape(n_dev, 32, DH)
        a_s[...] = both[:, :DH].reshape(n_dev, 32, DH)
        t_s[...] = both[:, DH:].reshape(n_dev, 32, DH)
        extra = []
        for n in range(5):
            if n < 4:
                dev = meta_ref[n, 0]
                kr, vr = (ok_ref, ov_ref) if n < 2 else (xk_ref, xv_ref)
                k, v = kr[n % 2, :, lanes], vr[n % 2, :, lanes]
                live = (row_req == meta_ref[n, 1]) & (lane < meta_ref[n, 2])
            else:
                dev = pre
                k, v = nk_ref[:, lanes], nv_ref[:, lanes]
                live = new_live
            s = lax.dot_general(q_ref[dev, qrows, :], k, NT, preferred_element_type=f32)
            s = jnp.where(live, s, NEG)
            peak = jnp.max(s, axis=1, keepdims=True)
            w = jnp.where(live, jnp.exp2((s - peak) * EXPO), 0.0).astype(bf16)
            o = jnp.dot(w, jnp.concatenate([v, ones], axis=1), preferred_element_type=f32)
            extra.append((dev, peak, o))
        for dev, peak, o in extra:
            old = m_s[dev]
            new = jnp.maximum(old, peak)
            fa = jnp.exp2((old - new) * EXPO)
            fb = jnp.exp2((peak - new) * EXPO)
            m_s[dev] = new
            a_s[dev] = a_s[dev] * fa + o[:, :DH] * fb
            t_s[dev] = t_s[dev] * fa + o[:, DH:] * fb
        total = t_s[...]
        out_ref[:, i * 32 : (i + 1) * 32, :] = a_s[...] / total
        l_s[:, i * 32 : (i + 1) * 32, :] = m_s[...] * EXPO + jnp.log(total) * LOG2E
    eye = lax.broadcasted_iota(jnp.int32, (DH, DH), 0) == lax.broadcasted_iota(jnp.int32, (DH, DH), 1)
    for dev in range(n_dev):
        line = jnp.sum(jnp.where(eye, l_s[dev], 0.0), axis=0, keepdims=True)
        out_ref[dev, 128:136, :] = jnp.broadcast_to(line, (8, DH))


def columns(lines):
    pad = jnp.zeros((DH - lines.shape[0], DH), f32)
    return jnp.concatenate([lines, pad], axis=0).T


def core_merge_kernel(a_ref, b_ref, out_ref):
    n_dev = a_ref.shape[0]
    la = a_ref[:, 128:136, :][:, 0, :]
    lb = b_ref[:, 128:136, :][:, 0, :]
    top = jnp.maximum(la, lb)
    wa = jnp.exp2(la - top)
    wb = jnp.exp2(lb - top)
    total = wa + wb
    lse = top + jnp.log(total) * LOG2E
    hi = lse.astype(bf16).astype(f32)
    mid = (lse - hi).astype(bf16).astype(f32)
    low = lse - hi - mid
    ca = columns(wa * (LIFT / total))
    cb = columns(wb * (LIFT / total))
    for dev in range(n_dev):
        out_ref[dev, 0:128, :] = (
            a_ref[dev, 0:128, :] * ca[:, dev : dev + 1] + b_ref[dev, 0:128, :] * cb[:, dev : dev + 1]
        )
        out_ref[dev, 128:136, :] = jnp.concatenate(
            [hi[dev : dev + 1], mid[dev : dev + 1], low[dev : dev + 1], jnp.zeros((5, DH), f32)], axis=0
        )


def final_kernel(z_ref, out_ref):
    n_dev = z_ref.shape[0]
    for c in range(2):
        lines = []
        for src in range(c, n_dev, 2):
            parts = z_ref[src, 128:136, :]
            lines.append(jnp.sum(parts, axis=0, keepdims=True))
        lse = jnp.concatenate(lines, axis=0)
        w = jnp.exp2(lse - jnp.max(lse, axis=0, keepdims=True))
        w = columns(w / (LIFT * jnp.sum(w, axis=0, keepdims=True)))
        o = 0.0
        for y, src in enumerate(range(c, n_dev, 2)):
            o = o + z_ref[src, 0:128, :] * w[:, y : y + 1]
        for h in range(H // 2):
            head = c * (H // 2) + h
            for s in range(2):
                r = h * 4 + s * 2
                out_ref[s, :, head * DH : (head + 1) * DH] = o[r : r + 2, :].astype(bf16)


def call(kernel, out_shape, ins, out_specs=VM, scratch=(), flops=0, moved=0, name=None, room=40):
    return pl.pallas_call(
        kernel,
        out_shape=out_shape,
        in_specs=ins,
        out_specs=out_specs,
        scratch_shapes=list(scratch),
        compiler_params=pltpu.CompilerParams(vmem_limit_bytes=room * 1024 * 1024),
        cost_estimate=pl.CostEstimate(flops=flops, bytes_accessed=moved, transcendentals=0),
        name=name,
    )


def per_device(
    queries,
    prefix_keys,
    prefix_values,
    pool_keys,
    pool_values,
    new_keys,
    new_values,
    block_table,
    suffix_lengths,
):
    n_req = lax.axis_size("req")
    n_pre = lax.axis_size("prefix")
    pair_rows = 4 * n_pre
    swap = [(i, i ^ 1) for i in range(n_req)]
    core = [(i, i ^ 1) for i in range(n_pre)]
    far_keys = lax.ppermute(pool_keys, "req", swap)
    far_values = lax.ppermute(pool_values, "req", swap)
    sds = jax.ShapeDtypeStruct
    own, nk, nv, meta = call(
        prepare_kernel,
        (sds((4 * H, DH), f32), sds((BLK, KVH * DH), bf16), sds((BLK, KVH * DH), bf16), sds((4, 3), jnp.int32)),
        [ANY] * 5,
        (VM, VM, VM, SM),
        [
            pltpu.VMEM(queries.shape, bf16),
            pltpu.VMEM(new_keys.shape, bf16),
            pltpu.VMEM(new_values.shape, bf16),
            pltpu.VMEM((suffix_lengths.size // 128, 128), jnp.int32),
            pltpu.VMEM((block_table.shape[1], 128), jnp.int32),
            pltpu.SemaphoreType.DMA((5,)),
        ],
        name="prepare",
        room=62,
    )(queries, new_keys, new_values, suffix_lengths.reshape(-1, 128), block_table.T)
    group = lax.all_gather(own.astype(jnp.float16), "prefix", axis=0)
    group = (group.astype(f32) * (1.0 / QLIFT)).astype(bf16)
    partial = sds((n_pre, 136, DH), f32)
    state = pltpu.VMEM((n_pre, 32, DH), f32)

    def attend(flip):
        return call(
            functools.partial(attend_kernel, flip),
            partial,
            [VM] * 9 + [SM],
            VM,
            [
                state,
                state,
                state,
                pltpu.VMEM((n_pre, 128, DH), f32),
            ],
            flops=800_000_000,
            moved=6_000_000,
            name="attend_other" if flip else "attend_own",
        )(group, prefix_keys, prefix_values, pool_keys, pool_values, far_keys, far_values, nk, nv, meta)

    theirs = lax.ppermute(attend(True), "prefix", core)
    mine = attend(False)
    merged = call(core_merge_kernel, partial, [VM, VM], moved=4_000_000, name="core_merge")(mine, theirs)
    spread = lax.all_to_all(merged.astype(jnp.float16), "prefix", 0, 0, tiled=True)
    return call(final_kernel, sds((2, 2, H * DH), bf16), [VM], moved=1_000_000, name="final")(
        spread.astype(f32)
    )


def solution(mesh):
    placed = (
        P(None, ("req", "prefix"), None),
        P("prefix", None),
        P("prefix", None),
        P(("req", "prefix"), None, None),
        P(("req", "prefix"), None, None),
        P(None, ("req", "prefix"), None),
        P(None, ("req", "prefix"), None),
        P(),
        P(),
    )
    return jax.shard_map(
        per_device,
        mesh=mesh,
        in_specs=placed,
        out_specs=P(None, ("req", "prefix"), None),
        check_vma=False,
    )
```

```python
import functools
import math

import jax
import jax.numpy as jnp
from jax import lax
from jax.experimental import pallas as pl
from jax.experimental.pallas import tpu as pltpu
from jax.sharding import PartitionSpec as P

H = 64
KVH = 8
DH = 128
BLK = 128
GROUP = H // KVH
HALF = KVH // 2
NEG = -1e30
LOG2E = 1.0 / math.log(2.0)
EXPO = LOG2E / math.sqrt(DH)
LIFT = 8192.0
QLIFT = 2048.0

bf16 = jnp.bfloat16
f32 = jnp.float32
NT = (((1,), (1,)), ((), ()))
VM = pl.BlockSpec(memory_space=pltpu.VMEM)
SM = pl.BlockSpec(memory_space=pltpu.SMEM)
ANY = pl.BlockSpec(memory_space=pl.ANY)


def prepare_kernel(
    q_ref, nk_ref, nv_ref, len_ref, table_ref, qt_ref, nkp_ref, nvp_ref, meta_ref,
    q_s, nk_s, nv_s, len_s, table_s, sems,
):
    req = lax.axis_index("req")
    pre = lax.axis_index("prefix")
    n_pre = lax.axis_size("prefix")
    pair_rows = 4 * n_pre
    per_line = 128 // pair_rows
    pair = req // 2
    side = req % 2
    line = pair // per_line
    first = (pair % per_line) * pair_rows
    lanes = pl.ds(pl.multiple_of(line * 128, 128), 128)
    sources = (len_ref, table_ref.at[:, lanes], q_ref, nk_ref, nv_ref)
    copies = [
        pltpu.make_async_copy(src, dst, sems.at[i])
        for i, (src, dst) in enumerate(zip(sources, (len_s, table_s, q_s, nk_s, nv_s)))
    ]
    for copy in copies:
        copy.start()
    for copy in copies:
        copy.wait()
    pieces = []
    steps = [q_s[s].astype(f32) * QLIFT for s in range(2)]
    for head in range(H):
        for s in range(2):
            pieces.append(steps[s][:, head * DH : (head + 1) * DH])
    qt_ref[...] = jnp.concatenate(pieces, axis=0)
    for src, dst in ((nk_s, nkp_ref), (nv_s, nvp_ref)):
        top = jnp.concatenate([src[0].astype(f32), src[1].astype(f32), jnp.zeros((12, KVH * DH), f32)], axis=0)
        dst[...] = jnp.zeros(dst.shape, bf16)
        dst[0:16, :] = top.astype(bf16)
    table = table_s[...]
    lane = lax.broadcasted_iota(jnp.int32, table.shape, 1) - first
    block = lax.broadcasted_iota(jnp.int32, table.shape, 0)
    left = jnp.broadcast_to(len_s[pl.ds(line, 1), :], table.shape) - block * BLK
    usable = (left > 0) & (lane >= 0) & (lane < pair_rows)
    for n in range(4):
        holder = side if n < 2 else 1 - side
        slot = (holder * n_pre + pre) * 2 + n % 2
        hit = (table == slot) & usable
        owner = jnp.sum(jnp.where(hit, lane, 0)) - side * (pair_rows // 2)
        live = jnp.sum(jnp.where(hit, jnp.minimum(left, BLK), 0))
        mine = (owner >= 0) & (owner < pair_rows // 2)
        owner = jnp.where(mine, owner, 0)
        meta_ref[n, 0] = owner // 2
        meta_ref[n, 1] = owner % 2
        meta_ref[n, 2] = jnp.where(mine, live, 0)


def attend_kernel(
    flip, q_ref, pk_ref, pv_ref, ok_ref, ov_ref, xk_ref, xv_ref, nk_ref, nv_ref, meta_ref, out_ref, m_s,
):
    pre = lax.axis_index("prefix")
    half = pre % 2
    if flip:
        half = 1 - half
    n_dev = q_ref.shape[0]
    rows = n_dev * 32
    ones = jnp.ones((16, BLK), bf16)
    key = lax.broadcasted_iota(jnp.int32, (BLK, DH), 0)
    lane = lax.broadcasted_iota(jnp.int32, (BLK, DH), 1)
    lane_dev, lane_req, lane_step = lane // 32, lane % 2, lane // 2 % 2
    n_blocks = pk_ref.shape[0] // BLK
    masks = []
    for n in range(4):
        limit = jnp.where((lane_dev == meta_ref[n, 0] % 4) & (lane_req == meta_ref[n, 1]), meta_ref[n, 2], 0)
        masks.append(key < limit)
    masks.append((lane_dev == pre % 4) & (key < 4) & (key % 2 == lane_req) & (key // 2 <= lane_step))
    for i in range(HALF):
        kvh = half * HALF + i
        lanes = pl.ds(pl.multiple_of(kvh * DH, DH), DH)
        qrows = pl.ds(pl.multiple_of(kvh * 32, 32), 32)
        q = q_ref[:, qrows, :].reshape(rows, DH)
        scores = lax.dot_general(pk_ref[:, lanes], q, NT, preferred_element_type=f32)
        peaks, outs = [], []
        for b in range(n_blocks):
            span = slice(b * BLK, (b + 1) * BLK)
            s = scores[span]
            peak = jnp.max(s, axis=0, keepdims=True)
            w = jnp.exp2((s - peak) * EXPO).astype(bf16)
            v = jnp.concatenate([pv_ref[span, lanes].T, ones], axis=0)
            peaks.append(peak)
            outs.append(jnp.dot(v, w, preferred_element_type=f32)[0:136])
        top = functools.reduce(jnp.maximum, peaks)
        both = 0.0
        for peak, o in zip(peaks, outs):
            both = both + jnp.exp2((peak - top) * EXPO) * o
        m_s[i : i + 1, :] = top
        out_ref[i] = both
        extra = []
        for n in range(5):
            if n < 4:
                kr, vr = (ok_ref, ov_ref) if n < 2 else (xk_ref, xv_ref)
                k, v = kr[n % 2, :, lanes], vr[n % 2, :, lanes]
                quad = meta_ref[n, 0] // 4
            else:
                k, v = nk_ref[:, lanes], nv_ref[:, lanes]
                quad = pre // 4
            qn = q_ref[pl.ds(quad * 4, 4), qrows, :].reshape(DH, DH)
            s = lax.dot_general(k, qn, NT, preferred_element_type=f32)
            s = jnp.where(masks[n], s, NEG)
            peak = jnp.max(s, axis=0, keepdims=True)
            w = jnp.where(masks[n], jnp.exp2((s - peak) * EXPO), 0.0).astype(bf16)
            o = jnp.dot(jnp.concatenate([v.T, ones], axis=0), w, preferred_element_type=f32)[0:136]
            extra.append((pl.ds(pl.multiple_of(quad * DH, DH), DH), peak, o))
        for at, peak, o in extra:
            old = m_s[i : i + 1, at]
            new = jnp.maximum(old, peak)
            m_s[i : i + 1, at] = new
            out_ref[i, :, at] = (
                out_ref[i, :, at] * jnp.exp2((old - new) * EXPO) + o * jnp.exp2((peak - new) * EXPO)
            )
        total = out_ref[i, 128:129, :]
        out_ref[i, 0:128, :] = out_ref[i, 0:128, :] * (1.0 / total)
        lse = m_s[i : i + 1, :] * EXPO + jnp.log(total) * LOG2E
        out_ref[i, 128:136, :] = jnp.broadcast_to(lse, (8, rows))


def core_merge_kernel(a_ref, b_ref, out_ref):
    rows = a_ref.shape[2]
    high, low = [], []
    for i in range(HALF):
        la = a_ref[i, 128:129, :]
        lb = b_ref[i, 128:129, :]
        top = jnp.maximum(la, lb)
        wa = jnp.exp2(la - top)
        wb = jnp.exp2(lb - top)
        total = wa + wb
        scale = LIFT / total
        o = a_ref[i, 0:128, :] * (wa * scale) + b_ref[i, 0:128, :] * (wb * scale)
        for quad in range(rows // DH):
            out_ref[quad * 4 : quad * 4 + 4, i * 32 : (i + 1) * 32, :] = (
                o[:, quad * DH : (quad + 1) * DH].T.reshape(4, 32, DH)
            )
        lse = top + jnp.log(total) * LOG2E
        far = lse * 8193.0
        head = far - (far - lse)
        high.append(head)
        low.append(lse - head)
    parts = jnp.concatenate(high + low, axis=0)
    for dev in range(rows // 32):
        out_ref[dev, 128:136, :] = parts[:, dev // 4 * DH : (dev // 4 + 1) * DH]


def final_kernel(z_ref, out_ref, w_s):
    n_dev = z_ref.shape[0]
    pre = lax.axis_index("prefix")
    mine = pl.ds(pl.multiple_of(pre % 4 * 32, 32), 32)
    for c in range(2):
        lses = []
        for src in range(c, n_dev, 2):
            parts = z_ref[src, 128:136, :]
            lses.append(parts[0:4] + parts[4:8])
        top = functools.reduce(jnp.maximum, lses)
        weights = [jnp.exp2(lse - top) for lse in lses]
        scale = 1.0 / (LIFT * sum(weights))
        lines = [w * scale for w in weights]
        lines.append(jnp.zeros((DH - 2 * n_dev, DH), f32))
        w_s[c] = jnp.concatenate(lines, axis=0).T
        columns = w_s[c, mine, :]
        for i in range(HALF):
            o = 0.0
            for y, src in enumerate(range(c, n_dev, 2)):
                o = o + z_ref[src, i * 32 : (i + 1) * 32, :] * columns[:, y * 4 + i : y * 4 + i + 1]
            for g in range(GROUP):
                head = (c * HALF + i) * GROUP + g
                for s in range(2):
                    r = g * 4 + s * 2
                    out_ref[s, :, head * DH : (head + 1) * DH] = o[r : r + 2, :].astype(bf16)


def call(kernel, out_shape, ins, out_specs=VM, scratch=(), flops=0, moved=0, name=None, room=40):
    return pl.pallas_call(
        kernel,
        out_shape=out_shape,
        in_specs=ins,
        out_specs=out_specs,
        scratch_shapes=list(scratch),
        compiler_params=pltpu.CompilerParams(vmem_limit_bytes=room * 1024 * 1024),
        cost_estimate=pl.CostEstimate(flops=flops, bytes_accessed=moved, transcendentals=0),
        name=name,
    )


def per_device(
    queries,
    prefix_keys,
    prefix_values,
    pool_keys,
    pool_values,
    new_keys,
    new_values,
    block_table,
    suffix_lengths,
):
    n_req = lax.axis_size("req")
    n_pre = lax.axis_size("prefix")
    pair_rows = 4 * n_pre
    swap = [(i, i ^ 1) for i in range(n_req)]
    core = [(i, i ^ 1) for i in range(n_pre)]
    far_keys = lax.ppermute(pool_keys, "req", swap)
    far_values = lax.ppermute(pool_values, "req", swap)
    sds = jax.ShapeDtypeStruct
    own, nk, nv, meta = call(
        prepare_kernel,
        (sds((4 * H, DH), f32), sds((BLK, KVH * DH), bf16), sds((BLK, KVH * DH), bf16), sds((4, 3), jnp.int32)),
        [ANY] * 5,
        (VM, VM, VM, SM),
        [
            pltpu.VMEM(queries.shape, bf16),
            pltpu.VMEM(new_keys.shape, bf16),
            pltpu.VMEM(new_values.shape, bf16),
            pltpu.VMEM((suffix_lengths.size // 128, 128), jnp.int32),
            pltpu.VMEM((block_table.shape[1], 128), jnp.int32),
            pltpu.SemaphoreType.DMA((5,)),
        ],
        name="prepare",
        room=62,
    )(queries, new_keys, new_values, suffix_lengths.reshape(-1, 128), block_table.T)
    group = lax.all_gather(own.astype(jnp.float16), "prefix", axis=0)
    group = (group.astype(f32) * (1.0 / QLIFT)).astype(bf16)
    rows = n_pre * 32

    def attend(flip):
        return call(
            functools.partial(attend_kernel, flip),
            sds((HALF, 136, rows), f32),
            [VM] * 9 + [SM],
            VM,
            [pltpu.VMEM((HALF, rows), f32)],
            flops=800_000_000,
            moved=6_000_000,
            name="attend_other" if flip else "attend_own",
        )(group, prefix_keys, prefix_values, pool_keys, pool_values, far_keys, far_values, nk, nv, meta)

    theirs = lax.ppermute(attend(True), "prefix", core)
    mine = attend(False)
    merged = call(core_merge_kernel, sds((n_pre, 136, DH), f32), [VM, VM], moved=4_000_000, name="core_merge")(
        mine, theirs
    )
    spread = lax.all_to_all(merged.astype(jnp.float16), "prefix", 0, 0, tiled=True)
    return call(
        final_kernel,
        sds((2, 2, H * DH), bf16),
        [VM],
        VM,
        [pltpu.VMEM((2, DH, DH), f32)],
        moved=1_000_000,
        name="final",
    )(spread.astype(f32))


def solution(mesh):
    placed = (
        P(None, ("req", "prefix"), None),
        P("prefix", None),
        P("prefix", None),
        P(("req", "prefix"), None, None),
        P(("req", "prefix"), None, None),
        P(None, ("req", "prefix"), None),
        P(None, ("req", "prefix"), None),
        P(),
        P(),
    )
    return jax.shard_map(
        per_device,
        mesh=mesh,
        in_specs=placed,
        out_specs=P(None, ("req", "prefix"), None),
        check_vma=False,
    )
```

```python
import functools
import math

import jax
import jax.numpy as jnp
from jax import lax
from jax.experimental import pallas as pl
from jax.experimental.pallas import tpu as pltpu
from jax.sharding import PartitionSpec as P

H = 64
KVH = 8
DH = 128
BLK = 128
GROUP = H // KVH
HALF = KVH // 2
NEG = -1e30
LOG2E = 1.0 / math.log(2.0)
EXPO = LOG2E / math.sqrt(DH)
LIFT = 8192.0
QLIFT = 2048.0

bf16 = jnp.bfloat16
f32 = jnp.float32
NT = (((1,), (1,)), ((), ()))
VM = pl.BlockSpec(memory_space=pltpu.VMEM)
SM = pl.BlockSpec(memory_space=pltpu.SMEM)
ANY = pl.BlockSpec(memory_space=pl.ANY)


def prepare_kernel(
    q_ref, nk_ref, nv_ref, len_ref, table_ref, qt_ref, nkp_ref, nvp_ref, meta_ref,
    q_s, nk_s, nv_s, len_s, table_s, sems,
):
    req = lax.axis_index("req")
    pre = lax.axis_index("prefix")
    n_pre = lax.axis_size("prefix")
    pair_rows = 4 * n_pre
    per_line = 128 // pair_rows
    pair = req // 2
    side = req % 2
    line = pair // per_line
    first = (pair % per_line) * pair_rows
    lanes = pl.ds(pl.multiple_of(line * 128, 128), 128)
    sources = (len_ref, table_ref.at[:, lanes], q_ref, nk_ref, nv_ref)
    copies = [
        pltpu.make_async_copy(src, dst, sems.at[i])
        for i, (src, dst) in enumerate(zip(sources, (len_s, table_s, q_s, nk_s, nv_s)))
    ]
    for copy in copies:
        copy.start()
    for copy in copies:
        copy.wait()
    pieces = []
    steps = [q_s[s].astype(f32) * QLIFT for s in range(2)]
    for head in range(H):
        for s in range(2):
            pieces.append(steps[s][:, head * DH : (head + 1) * DH])
    qt_ref[...] = jnp.concatenate(pieces, axis=0)
    for src, dst in ((nk_s, nkp_ref), (nv_s, nvp_ref)):
        top = jnp.concatenate([src[0].astype(f32), src[1].astype(f32), jnp.zeros((12, KVH * DH), f32)], axis=0)
        dst[...] = top.astype(bf16)
    table = table_s[...]
    lane = lax.broadcasted_iota(jnp.int32, table.shape, 1) - first
    block = lax.broadcasted_iota(jnp.int32, table.shape, 0)
    left = jnp.broadcast_to(len_s[pl.ds(line, 1), :], table.shape) - block * BLK
    usable = (left > 0) & (lane >= 0) & (lane < pair_rows)
    for n in range(4):
        holder = side if n < 2 else 1 - side
        slot = (holder * n_pre + pre) * 2 + n % 2
        hit = (table == slot) & usable
        owner = jnp.sum(jnp.where(hit, lane, 0)) - side * (pair_rows // 2)
        live = jnp.sum(jnp.where(hit, jnp.minimum(left, BLK), 0))
        mine = (owner >= 0) & (owner < pair_rows // 2)
        owner = jnp.where(mine, owner, 0)
        meta_ref[n, 0] = owner // 2
        meta_ref[n, 1] = owner % 2
        meta_ref[n, 2] = jnp.where(mine, live, 0)


def attend_kernel(
    flip, q_ref, pk_ref, pv_ref, ok_ref, ov_ref, xk_ref, xv_ref, nk_ref, nv_ref, meta_ref, out_ref,
):
    pre = lax.axis_index("prefix")
    half = pre % 2
    if flip:
        half = 1 - half
    n_dev = q_ref.shape[0]
    rows = n_dev * 32
    n_quads = n_dev // 4
    n_blocks = pk_ref.shape[0] // BLK
    ones = jnp.ones((16, BLK), bf16)
    first = half * HALF

    def head_lanes(i):
        return pl.ds(pl.multiple_of((first + i) * DH, DH), DH)

    key = lax.broadcasted_iota(jnp.int32, (BLK, DH), 0)
    lane = lax.broadcasted_iota(jnp.int32, (BLK, DH), 1)
    lane_head, lane_req, lane_step = lane // 32, lane % 2, lane // 2 % 2
    own_rows = pl.ds(pl.multiple_of(first * 32, DH), DH)
    extra = []
    for n in range(5):
        if n < 4:
            kr, vr = (ok_ref, ov_ref) if n < 2 else (xk_ref, xv_ref)
            ks = [kr[n % 2, :, head_lanes(i)] for i in range(HALF)]
            vs = [vr[n % 2, :, head_lanes(i)].T for i in range(HALF)]
            dev = meta_ref[n, 0]
            live = key < jnp.where(lane_req == meta_ref[n, 1], meta_ref[n, 2], 0)
        else:
            ks = [nk_ref[:, head_lanes(i)] for i in range(HALF)]
            fill = jnp.zeros((BLK - HALF * 16, DH), bf16)
            vs = [jnp.concatenate([nv_ref[:, head_lanes(i)] for i in range(HALF)] + [fill], axis=0).T]
            dev = pre
            live = ((key < 4) & (key % 2 == lane_req) & (key // 2 <= lane_step))[0:16]
        count = ks[0].shape[0]
        every = lax.dot_general(
            jnp.concatenate(ks, axis=0), q_ref[dev, own_rows, :], NT, preferred_element_type=f32
        )
        s = every[0:count]
        for i in range(1, HALF):
            s = jnp.where(lane_head[0:count] == i, every[i * count : (i + 1) * count], s)
        s = jnp.where(live, s, NEG)
        peak = jnp.max(s, axis=0, keepdims=True)
        w = jnp.where(live, jnp.exp2((s - peak) * EXPO), 0.0)
        ws = [jnp.where(lane_head[0:count] == i, w, 0.0).astype(bf16) for i in range(HALF)]
        if n == 4:
            ws.append(fill)
        v = jnp.concatenate([jnp.concatenate(vs, axis=1), jnp.concatenate([ones] * len(vs), axis=1)], axis=0)
        o = jnp.dot(v, jnp.concatenate(ws, axis=0), preferred_element_type=f32)[0:136]
        extra.append((dev, peak, o))

    spot = lax.broadcasted_iota(jnp.int32, (1, rows), 1) // 32
    for i in range(HALF):
        lanes = head_lanes(i)
        qrows = pl.ds(pl.multiple_of((first + i) * 32, 32), 32)
        q = q_ref[:, qrows, :].reshape(rows, DH)
        scores = lax.dot_general(pk_ref[:, lanes], q, NT, preferred_element_type=f32)
        peaks, outs = [], []
        for b in range(n_blocks):
            span = slice(b * BLK, (b + 1) * BLK)
            s = scores[span]
            peak = jnp.max(s, axis=0, keepdims=True)
            w = jnp.exp2((s - peak) * EXPO).astype(bf16)
            v = jnp.concatenate([pv_ref[span, lanes].T, ones], axis=0)
            peaks.append(peak)
            outs.append(jnp.dot(v, w, preferred_element_type=f32)[0:136])
        wides = []
        for dev, peak, o in extra:
            turn = (dev + (4 - i)) % 4 * 32
            moved = pltpu.roll(peak, turn, 1)
            wides.append(jnp.where(spot == dev, jnp.concatenate([moved] * n_quads, axis=1), NEG))
        top = functools.reduce(jnp.maximum, peaks + wides)
        both = 0.0
        for peak, o in zip(peaks, outs):
            both = both + jnp.exp2((peak - top) * EXPO) * o
        out_ref[i] = both
        for (dev, peak, o), wide in zip(extra, wides):
            turn = (dev + (4 - i)) % 4 * 32
            f = jnp.exp2((wide - top) * EXPO)
            f = sum(f[:, quad * DH : (quad + 1) * DH] for quad in range(n_quads))
            at = pl.ds(pl.multiple_of(dev // 4 * DH, DH), DH)
            out_ref[i, :, at] = out_ref[i, :, at] + pltpu.roll(o, turn, 1) * f
        total = out_ref[i, 128:129, :]
        out_ref[i, 0:128, :] = out_ref[i, 0:128, :] * (1.0 / total)
        lse = top * EXPO + jnp.log(total) * LOG2E
        out_ref[i, 128:136, :] = jnp.broadcast_to(lse, (8, rows))


def core_merge_kernel(a_ref, b_ref, out_ref):
    rows = a_ref.shape[2]
    high, low = [], []
    for i in range(HALF):
        la = a_ref[i, 128:129, :]
        lb = b_ref[i, 128:129, :]
        top = jnp.maximum(la, lb)
        wa = jnp.exp2(la - top)
        wb = jnp.exp2(lb - top)
        total = wa + wb
        scale = LIFT / total
        o = a_ref[i, 0:128, :] * (wa * scale) + b_ref[i, 0:128, :] * (wb * scale)
        for quad in range(rows // DH):
            out_ref[quad * 4 : quad * 4 + 4, i * 32 : (i + 1) * 32, :] = (
                o[:, quad * DH : (quad + 1) * DH].T.reshape(4, 32, DH)
            )
        lse = top + jnp.log(total) * LOG2E
        far = lse * 8193.0
        head = far - (far - lse)
        high.append(head)
        low.append(lse - head)
    parts = jnp.concatenate(high + low, axis=0)
    for dev in range(rows // 32):
        out_ref[dev, 128:136, :] = parts[:, dev // 4 * DH : (dev // 4 + 1) * DH]


def final_kernel(z_ref, out_ref, w_s):
    n_dev = z_ref.shape[0]
    pre = lax.axis_index("prefix")
    mine = pl.ds(pl.multiple_of(pre % 4 * 32, 32), 32)
    for c in range(2):
        lses = []
        for src in range(c, n_dev, 2):
            parts = z_ref[src, 128:136, :]
            lses.append(parts[0:4] + parts[4:8])
        top = functools.reduce(jnp.maximum, lses)
        weights = [jnp.exp2(lse - top) for lse in lses]
        scale = 1.0 / (LIFT * sum(weights))
        lines = [w * scale for w in weights]
        lines.append(jnp.zeros((DH - 2 * n_dev, DH), f32))
        w_s[c] = jnp.concatenate(lines, axis=0).T
        columns = w_s[c, mine, :]
        for i in range(HALF):
            o = 0.0
            for y, src in enumerate(range(c, n_dev, 2)):
                o = o + z_ref[src, i * 32 : (i + 1) * 32, :] * columns[:, y * 4 + i : y * 4 + i + 1]
            for g in range(GROUP):
                head = (c * HALF + i) * GROUP + g
                for s in range(2):
                    r = g * 4 + s * 2
                    out_ref[s, :, head * DH : (head + 1) * DH] = o[r : r + 2, :].astype(bf16)


def call(kernel, out_shape, ins, out_specs=VM, scratch=(), flops=0, moved=0, name=None, room=40):
    return pl.pallas_call(
        kernel,
        out_shape=out_shape,
        in_specs=ins,
        out_specs=out_specs,
        scratch_shapes=list(scratch),
        compiler_params=pltpu.CompilerParams(vmem_limit_bytes=room * 1024 * 1024),
        cost_estimate=pl.CostEstimate(flops=flops, bytes_accessed=moved, transcendentals=0),
        name=name,
    )


def per_device(
    queries,
    prefix_keys,
    prefix_values,
    pool_keys,
    pool_values,
    new_keys,
    new_values,
    block_table,
    suffix_lengths,
):
    n_req = lax.axis_size("req")
    n_pre = lax.axis_size("prefix")
    pair_rows = 4 * n_pre
    swap = [(i, i ^ 1) for i in range(n_req)]
    core = [(i, i ^ 1) for i in range(n_pre)]
    far_keys = lax.ppermute(pool_keys, "req", swap)
    far_values = lax.ppermute(pool_values, "req", swap)
    sds = jax.ShapeDtypeStruct
    own, nk, nv, meta = call(
        prepare_kernel,
        (sds((4 * H, DH), f32), sds((16, KVH * DH), bf16), sds((16, KVH * DH), bf16), sds((4, 3), jnp.int32)),
        [ANY] * 5,
        (VM, VM, VM, SM),
        [
            pltpu.VMEM(queries.shape, bf16),
            pltpu.VMEM(new_keys.shape, bf16),
            pltpu.VMEM(new_values.shape, bf16),
            pltpu.VMEM((suffix_lengths.size // 128, 128), jnp.int32),
            pltpu.VMEM((block_table.shape[1], 128), jnp.int32),
            pltpu.SemaphoreType.DMA((5,)),
        ],
        name="prepare",
        room=62,
    )(queries, new_keys, new_values, suffix_lengths.reshape(-1, 128), block_table.T)
    group = lax.all_gather(own.astype(jnp.float16), "prefix", axis=0)
    group = (group.astype(f32) * (1.0 / QLIFT)).astype(bf16)
    rows = n_pre * 32

    def attend(flip):
        return call(
            functools.partial(attend_kernel, flip),
            sds((HALF, 136, rows), f32),
            [VM] * 9 + [SM],
            flops=800_000_000,
            moved=6_000_000,
            name="attend_other" if flip else "attend_own",
        )(group, prefix_keys, prefix_values, pool_keys, pool_values, far_keys, far_values, nk, nv, meta)

    theirs = lax.ppermute(attend(True), "prefix", core)
    mine = attend(False)
    merged = call(core_merge_kernel, sds((n_pre, 136, DH), f32), [VM, VM], moved=4_000_000, name="core_merge")(
        mine, theirs
    )
    spread = lax.all_to_all(merged.astype(jnp.float16), "prefix", 0, 0, tiled=True)
    return call(
        final_kernel,
        sds((2, 2, H * DH), bf16),
        [VM],
        VM,
        [pltpu.VMEM((2, DH, DH), f32)],
        moved=1_000_000,
        name="final",
    )(spread.astype(f32))


def solution(mesh):
    placed = (
        P(None, ("req", "prefix"), None),
        P("prefix", None),
        P("prefix", None),
        P(("req", "prefix"), None, None),
        P(("req", "prefix"), None, None),
        P(None, ("req", "prefix"), None),
        P(None, ("req", "prefix"), None),
        P(),
        P(),
    )
    return jax.shard_map(
        per_device,
        mesh=mesh,
        in_specs=placed,
        out_specs=P(None, ("req", "prefix"), None),
        check_vma=False,
    )
```

```python
import functools
import math

import jax
import jax.numpy as jnp
from jax import lax
from jax.experimental import pallas as pl
from jax.experimental.pallas import tpu as pltpu
from jax.sharding import PartitionSpec as P

H = 64
KVH = 8
DH = 128
BLK = 128
GROUP = H // KVH
HALF = KVH // 2
NEG = -1e30
LOG2E = 1.0 / math.log(2.0)
EXPO = LOG2E / math.sqrt(DH)
LIFT = 8192.0
QLIFT = 2048.0

bf16 = jnp.bfloat16
f32 = jnp.float32
NT = (((1,), (1,)), ((), ()))
VM = pl.BlockSpec(memory_space=pltpu.VMEM)
SM = pl.BlockSpec(memory_space=pltpu.SMEM)


def find_owners(len_ref, table_ref, meta_ref):
    req = lax.axis_index("req")
    pre = lax.axis_index("prefix")
    n_pre = lax.axis_size("prefix")
    pair_rows = 4 * n_pre
    per_line = 128 // pair_rows
    pair = req // 2
    side = req % 2
    line = pair // per_line
    first = (pair % per_line) * pair_rows
    table = table_ref[:, pl.ds(pl.multiple_of(line * 128, 128), 128)]
    lane = lax.broadcasted_iota(jnp.int32, table.shape, 1) - first
    block = lax.broadcasted_iota(jnp.int32, table.shape, 0)
    left = jnp.broadcast_to(len_ref[pl.ds(line, 1), :], table.shape) - block * BLK
    usable = (left > 0) & (lane >= 0) & (lane < pair_rows)
    for n in range(4):
        holder = side if n < 2 else 1 - side
        slot = (holder * n_pre + pre) * 2 + n % 2
        hit = (table == slot) & usable
        found = jnp.sum(jnp.where(hit, lane * 256 + jnp.minimum(left, BLK), 0))
        owner = found // 256 - side * (pair_rows // 2)
        mine = (owner >= 0) & (owner < pair_rows // 2)
        owner = jnp.where(mine, owner, 0)
        meta_ref[n, 0] = owner // 2
        meta_ref[n, 1] = owner % 2
        meta_ref[n, 2] = jnp.where(mine, found % 256, 0)


def attend_kernel(
    flip, q_ref, pk_ref, pv_ref, ok_ref, ov_ref, xk_ref, xv_ref, nk_ref, nv_ref, *refs
):
    pre = lax.axis_index("prefix")
    half = pre % 2
    if flip:
        half = 1 - half
        len_ref, table_ref, out_ref, meta_ref = refs
        find_owners(len_ref, table_ref, meta_ref)
    else:
        meta_ref, out_ref = refs
    n_dev = q_ref.shape[0]
    rows = n_dev * 32
    n_quads = n_dev // 4
    n_blocks = pk_ref.shape[0] // BLK
    ones = jnp.ones((16, BLK), bf16)
    first = half * HALF

    def head_lanes(i):
        return pl.ds(pl.multiple_of((first + i) * DH, DH), DH)

    def tokens(ref, i):
        pair = [ref[s, :, head_lanes(i)].astype(f32) for s in range(2)]
        return jnp.concatenate(pair + [jnp.zeros((12, DH), f32)], axis=0).astype(bf16)

    key = lax.broadcasted_iota(jnp.int32, (BLK, DH), 0)
    lane = lax.broadcasted_iota(jnp.int32, (BLK, DH), 1)
    lane_head, lane_req, lane_step = lane // 32, lane % 2, lane // 2 % 2
    own_rows = pl.ds(pl.multiple_of(first * 32, DH), DH)
    extra = []
    for n in range(5):
        if n < 4:
            kr, vr = (ok_ref, ov_ref) if n < 2 else (xk_ref, xv_ref)
            ks = [kr[n % 2, :, head_lanes(i)] for i in range(HALF)]
            vs = [vr[n % 2, :, head_lanes(i)].T for i in range(HALF)]
            dev = meta_ref[n, 0]
            live = key < jnp.where(lane_req == meta_ref[n, 1], meta_ref[n, 2], 0)
        else:
            ks = [tokens(nk_ref, i) for i in range(HALF)]
            fill = jnp.zeros((BLK - HALF * 16, DH), bf16)
            vs = [jnp.concatenate([tokens(nv_ref, i) for i in range(HALF)] + [fill], axis=0).T]
            dev = pre
            live = ((key < 4) & (key % 2 == lane_req) & (key // 2 <= lane_step))[0:16]
        count = ks[0].shape[0]
        every = lax.dot_general(
            jnp.concatenate(ks, axis=0), q_ref[dev, own_rows, :], NT, preferred_element_type=f32
        )
        s = every[0:count]
        for i in range(1, HALF):
            s = jnp.where(lane_head[0:count] == i, every[i * count : (i + 1) * count], s)
        s = jnp.where(live, s, NEG)
        peak = jnp.max(s, axis=0, keepdims=True)
        w = jnp.where(live, jnp.exp2((s - peak) * EXPO), 0.0)
        ws = [jnp.where(lane_head[0:count] == i, w, 0.0).astype(bf16) for i in range(HALF)]
        if n == 4:
            ws.append(fill)
        v = jnp.concatenate([jnp.concatenate(vs, axis=1), jnp.concatenate([ones] * len(vs), axis=1)], axis=0)
        o = jnp.dot(v, jnp.concatenate(ws, axis=0), preferred_element_type=f32)[0:136]
        extra.append((dev, peak, o))

    spot = lax.broadcasted_iota(jnp.int32, (1, rows), 1) // 32
    for i in range(HALF):
        lanes = head_lanes(i)
        qrows = pl.ds(pl.multiple_of((first + i) * 32, 32), 32)
        q = q_ref[:, qrows, :].reshape(rows, DH)
        scores = lax.dot_general(pk_ref[:, lanes], q, NT, preferred_element_type=f32)
        peaks, outs = [], []
        for b in range(n_blocks):
            span = slice(b * BLK, (b + 1) * BLK)
            s = scores[span]
            peak = jnp.max(s, axis=0, keepdims=True)
            w = jnp.exp2((s - peak) * EXPO).astype(bf16)
            v = jnp.concatenate([pv_ref[span, lanes].T, ones], axis=0)
            peaks.append(peak)
            outs.append(jnp.dot(v, w, preferred_element_type=f32)[0:136])
        wides = []
        for dev, peak, o in extra:
            turn = (dev + (4 - i)) % 4 * 32
            moved = pltpu.roll(peak, turn, 1)
            wides.append(jnp.where(spot == dev, jnp.concatenate([moved] * n_quads, axis=1), NEG))
        top = functools.reduce(jnp.maximum, peaks + wides)
        both = 0.0
        for peak, o in zip(peaks, outs):
            both = both + jnp.exp2((peak - top) * EXPO) * o
        out_ref[i] = both
        for (dev, peak, o), wide in zip(extra, wides):
            turn = (dev + (4 - i)) % 4 * 32
            f = jnp.exp2((wide - top) * EXPO)
            f = sum(f[:, quad * DH : (quad + 1) * DH] for quad in range(n_quads))
            at = pl.ds(pl.multiple_of(dev // 4 * DH, DH), DH)
            out_ref[i, :, at] = out_ref[i, :, at] + pltpu.roll(o, turn, 1) * f
        out_ref[i, 132:136, :] = jnp.broadcast_to(top * EXPO, (4, rows))


def core_merge_kernel(a_ref, b_ref, out_ref):
    rows = a_ref.shape[2]
    high, low = [], []
    for i in range(HALF):
        pa = a_ref[i, 132:133, :]
        pb = b_ref[i, 132:133, :]
        top = jnp.maximum(pa, pb)
        wa = jnp.exp2(pa - top)
        wb = jnp.exp2(pb - top)
        total = a_ref[i, 128:129, :] * wa + b_ref[i, 128:129, :] * wb
        scale = LIFT / total
        o = a_ref[i, 0:128, :] * (wa * scale) + b_ref[i, 0:128, :] * (wb * scale)
        for quad in range(rows // DH):
            out_ref[quad * 4 : quad * 4 + 4, i * 32 : (i + 1) * 32, :] = (
                o[:, quad * DH : (quad + 1) * DH].T.reshape(4, 32, DH)
            )
        lse = top + jnp.log(total) * LOG2E
        far = lse * 8193.0
        head = far - (far - lse)
        high.append(head)
        low.append(lse - head)
    parts = jnp.concatenate(high + low, axis=0)
    for dev in range(rows // 32):
        out_ref[dev, 128:136, :] = parts[:, dev // 4 * DH : (dev // 4 + 1) * DH]


def final_kernel(z_ref, out_ref, w_s):
    n_dev = z_ref.shape[0]
    pre = lax.axis_index("prefix")
    mine = pl.ds(pl.multiple_of(pre % 4 * 32, 32), 32)
    for c in range(2):
        lses = []
        for src in range(c, n_dev, 2):
            parts = z_ref[src, 128:136, :]
            lses.append(parts[0:4] + parts[4:8])
        top = functools.reduce(jnp.maximum, lses)
        weights = [jnp.exp2(lse - top) for lse in lses]
        scale = 1.0 / (LIFT * sum(weights))
        lines = [w * scale for w in weights]
        lines.append(jnp.zeros((DH - 2 * n_dev, DH), f32))
        w_s[c] = jnp.concatenate(lines, axis=0).T
        columns = w_s[c, mine, :]
        for i in range(HALF):
            o = 0.0
            for y, src in enumerate(range(c, n_dev, 2)):
                o = o + z_ref[src, i * 32 : (i + 1) * 32, :] * columns[:, y * 4 + i : y * 4 + i + 1]
            for g in range(GROUP):
                head = (c * HALF + i) * GROUP + g
                for s in range(2):
                    r = g * 4 + s * 2
                    out_ref[s, :, head * DH : (head + 1) * DH] = o[r : r + 2, :].astype(bf16)


def call(kernel, out_shape, ins, out_specs=VM, scratch=(), flops=0, moved=0, name=None):
    return pl.pallas_call(
        kernel,
        out_shape=out_shape,
        in_specs=ins,
        out_specs=out_specs,
        scratch_shapes=list(scratch),
        compiler_params=pltpu.CompilerParams(vmem_limit_bytes=40 * 1024 * 1024),
        cost_estimate=pl.CostEstimate(flops=flops, bytes_accessed=moved, transcendentals=0),
        name=name,
    )


def per_device(
    queries,
    prefix_keys,
    prefix_values,
    pool_keys,
    pool_values,
    new_keys,
    new_values,
    block_table,
    suffix_lengths,
):
    n_req = lax.axis_size("req")
    n_pre = lax.axis_size("prefix")
    swap = [(i, i ^ 1) for i in range(n_req)]
    core = [(i, i ^ 1) for i in range(n_pre)]
    far_keys = lax.ppermute(pool_keys, "req", swap)
    far_values = lax.ppermute(pool_values, "req", swap)
    sds = jax.ShapeDtypeStruct
    own = (queries.astype(f32) * QLIFT).astype(jnp.float16)
    own = own.reshape(4, H, DH).transpose(1, 0, 2).reshape(4 * H, DH)
    group = lax.all_gather(own, "prefix", axis=0)
    group = (group.astype(f32) * (1.0 / QLIFT)).astype(bf16)
    rows = n_pre * 32

    common = (
        group, prefix_keys, prefix_values, pool_keys, pool_values, far_keys, far_values, new_keys, new_values
    )
    part = sds((HALF, 136, rows), f32)
    cost = dict(flops=800_000_000, moved=6_000_000)
    other, meta = call(
        functools.partial(attend_kernel, True),
        (part, sds((4, 3), jnp.int32)),
        [VM] * 11,
        (VM, SM),
        name="attend_other",
        **cost,
    )(*common, suffix_lengths.reshape(-1, 128), block_table.T)
    theirs = lax.ppermute(other, "prefix", core)
    mine = call(
        functools.partial(attend_kernel, False), part, [VM] * 9 + [SM], name="attend_own", **cost
    )(*common, meta)
    merged = call(core_merge_kernel, sds((n_pre, 136, DH), f32), [VM, VM], moved=4_000_000, name="core_merge")(
        mine, theirs
    )
    spread = lax.all_to_all(merged.astype(jnp.float16), "prefix", 0, 0, tiled=True)
    return call(
        final_kernel,
        sds((2, 2, H * DH), bf16),
        [VM],
        VM,
        [pltpu.VMEM((2, DH, DH), f32)],
        moved=1_000_000,
        name="final",
    )(spread.astype(f32))


def solution(mesh):
    placed = (
        P(None, ("req", "prefix"), None),
        P("prefix", None),
        P("prefix", None),
        P(("req", "prefix"), None, None),
        P(("req", "prefix"), None, None),
        P(None, ("req", "prefix"), None),
        P(None, ("req", "prefix"), None),
        P(),
        P(),
    )
    return jax.shard_map(
        per_device,
        mesh=mesh,
        in_specs=placed,
        out_specs=P(None, ("req", "prefix"), None),
        check_vma=False,
    )
```

```python
import functools
import math

import jax
import jax.numpy as jnp
from jax import lax
from jax.experimental import pallas as pl
from jax.experimental.pallas import tpu as pltpu
from jax.sharding import PartitionSpec as P

H = 64
KVH = 8
DH = 128
BLK = 128
GROUP = H // KVH
HALF = KVH // 2
NEG = -1e30
LOG2E = 1.0 / math.log(2.0)
EXPO = LOG2E / math.sqrt(DH)
LIFT = 8192.0
QLIFT = 2048.0

bf16 = jnp.bfloat16
f32 = jnp.float32
NT = (((1,), (1,)), ((), ()))
VM = pl.BlockSpec(memory_space=pltpu.VMEM)
SM = pl.BlockSpec(memory_space=pltpu.SMEM)


def find_owners(len_ref, table_ref, meta_ref):
    req = lax.axis_index("req")
    pre = lax.axis_index("prefix")
    n_pre = lax.axis_size("prefix")
    pair_rows = 4 * n_pre
    per_line = 128 // pair_rows
    pair = req // 2
    side = req % 2
    line = pair // per_line
    first = (pair % per_line) * pair_rows
    table = table_ref[:, pl.ds(pl.multiple_of(line * 128, 128), 128)]
    lane = lax.broadcasted_iota(jnp.int32, table.shape, 1) - first
    block = lax.broadcasted_iota(jnp.int32, table.shape, 0)
    left = jnp.broadcast_to(len_ref[pl.ds(line, 1), :], table.shape) - block * BLK
    usable = (left > 0) & (lane >= 0) & (lane < pair_rows)
    for n in range(4):
        holder = side if n < 2 else 1 - side
        slot = (holder * n_pre + pre) * 2 + n % 2
        hit = (table == slot) & usable
        found = jnp.sum(jnp.where(hit, lane * 256 + jnp.minimum(left, BLK), 0))
        owner = found // 256 - side * (pair_rows // 2)
        mine = (owner >= 0) & (owner < pair_rows // 2)
        owner = jnp.where(mine, owner, 0)
        meta_ref[n, 0] = owner // 2
        meta_ref[n, 1] = owner % 2
        meta_ref[n, 2] = jnp.where(mine, found % 256, 0)


def attend_kernel(
    flip, q_ref, pk_ref, pv_ref, ok_ref, ov_ref, xk_ref, xv_ref, nk_ref, nv_ref, *refs
):
    pre = lax.axis_index("prefix")
    half = pre % 2
    if flip:
        half = 1 - half
        len_ref, table_ref, out_ref, meta_ref = refs
        find_owners(len_ref, table_ref, meta_ref)
    else:
        meta_ref, out_ref = refs
    n_dev = q_ref.shape[0]
    rows = n_dev * 32
    n_quads = n_dev // 4
    n_blocks = pk_ref.shape[0] // BLK
    ones = jnp.ones((16, BLK), bf16)
    first = half * HALF

    def head_lanes(i):
        return pl.ds(pl.multiple_of((first + i) * DH, DH), DH)

    def tokens(ref, i):
        pair = [ref[s, :, head_lanes(i)].astype(f32) for s in range(2)]
        return jnp.concatenate(pair + [jnp.zeros((12, DH), f32)], axis=0).astype(bf16)

    def products(i):
        q = q_ref[:, pl.ds(pl.multiple_of((first + i) * 32, 32), 32), :].reshape(rows, DH)
        return lax.dot_general(pk_ref[:, head_lanes(i)], q, NT, preferred_element_type=f32)

    def weigh(scores):
        peaks, ws = [], []
        for b in range(n_blocks):
            s = scores[b * BLK : (b + 1) * BLK]
            peak = jnp.max(s, axis=0, keepdims=True)
            ws.append(jnp.exp2((s - peak) * EXPO).astype(bf16))
            peaks.append(peak)
        return peaks, ws

    def collect(i, ws):
        outs = []
        for b in range(n_blocks):
            v = jnp.concatenate([pv_ref[b * BLK : (b + 1) * BLK, head_lanes(i)].T, ones], axis=0)
            outs.append(jnp.dot(v, ws[b], preferred_element_type=f32)[0:136])
        return outs

    key = lax.broadcasted_iota(jnp.int32, (BLK, DH), 0)
    lane = lax.broadcasted_iota(jnp.int32, (BLK, DH), 1)
    lane_head, lane_req, lane_step = lane // 32, lane % 2, lane // 2 % 2
    own_rows = pl.ds(pl.multiple_of(first * 32, DH), DH)
    stage = []
    for n in range(5):
        if n < 4:
            kr, vr = (ok_ref, ov_ref) if n < 2 else (xk_ref, xv_ref)
            ks = [kr[n % 2, :, head_lanes(i)] for i in range(HALF)]
            vs = [vr[n % 2, :, head_lanes(i)].T for i in range(HALF)]
            dev = meta_ref[n, 0]
            live = key < jnp.where(lane_req == meta_ref[n, 1], meta_ref[n, 2], 0)
        else:
            ks = [tokens(nk_ref, i) for i in range(HALF)]
            fill = jnp.zeros((BLK - HALF * 16, DH), bf16)
            vs = [jnp.concatenate([tokens(nv_ref, i) for i in range(HALF)] + [fill], axis=0).T]
            dev = pre
            live = ((key < 4) & (key % 2 == lane_req) & (key // 2 <= lane_step))[0:16]
        count = ks[0].shape[0]
        every = lax.dot_general(
            jnp.concatenate(ks, axis=0), q_ref[dev, own_rows, :], NT, preferred_element_type=f32
        )
        stage.append((n, vs, dev, live, count, every))
    scores = [products(i) for i in range(HALF)]
    weighed = []
    for n, vs, dev, live, count, every in stage:
        s = every[0:count]
        for i in range(1, HALF):
            s = jnp.where(lane_head[0:count] == i, every[i * count : (i + 1) * count], s)
        s = jnp.where(live, s, NEG)
        peak = jnp.max(s, axis=0, keepdims=True)
        w = jnp.where(live, jnp.exp2((s - peak) * EXPO), 0.0)
        ws = [jnp.where(lane_head[0:count] == i, w, 0.0).astype(bf16) for i in range(HALF)]
        if n == 4:
            ws.append(fill)
        v = jnp.concatenate([jnp.concatenate(vs, axis=1), jnp.concatenate([ones] * len(vs), axis=1)], axis=0)
        weighed.append((dev, peak, v, ws))
    extra = []
    for dev, peak, v, ws in weighed:
        o = jnp.dot(v, jnp.concatenate(ws, axis=0), preferred_element_type=f32)[0:136]
        extra.append((dev, peak, o))

    spot = lax.broadcasted_iota(jnp.int32, (1, rows), 1) // 32
    ready = weigh(scores[0])
    for i in range(HALF):
        peaks, ws = ready
        outs = collect(i, ws)
        if i + 1 < HALF:
            ready = weigh(scores[i + 1])
        wides = []
        for dev, peak, o in extra:
            turn = (dev + (4 - i)) % 4 * 32
            moved = pltpu.roll(peak, turn, 1)
            wides.append(jnp.where(spot == dev, jnp.concatenate([moved] * n_quads, axis=1), NEG))
        top = functools.reduce(jnp.maximum, peaks + wides)
        both = 0.0
        for peak, o in zip(peaks, outs):
            both = both + jnp.exp2((peak - top) * EXPO) * o
        out_ref[i] = both
        for (dev, peak, o), wide in zip(extra, wides):
            turn = (dev + (4 - i)) % 4 * 32
            f = jnp.exp2((wide - top) * EXPO)
            f = sum(f[:, quad * DH : (quad + 1) * DH] for quad in range(n_quads))
            at = pl.ds(pl.multiple_of(dev // 4 * DH, DH), DH)
            out_ref[i, :, at] = out_ref[i, :, at] + pltpu.roll(o, turn, 1) * f
        out_ref[i, 132:136, :] = jnp.broadcast_to(top * EXPO, (4, rows))


def core_merge_kernel(a_ref, b_ref, out_ref):
    rows = a_ref.shape[2]
    high, low = [], []
    for i in range(HALF):
        pa = a_ref[i, 132:133, :]
        pb = b_ref[i, 132:133, :]
        top = jnp.maximum(pa, pb)
        wa = jnp.exp2(pa - top)
        wb = jnp.exp2(pb - top)
        total = a_ref[i, 128:129, :] * wa + b_ref[i, 128:129, :] * wb
        scale = LIFT / total
        o = a_ref[i, 0:128, :] * (wa * scale) + b_ref[i, 0:128, :] * (wb * scale)
        for quad in range(rows // DH):
            out_ref[quad * 4 : quad * 4 + 4, i * 32 : (i + 1) * 32, :] = (
                o[:, quad * DH : (quad + 1) * DH].T.reshape(4, 32, DH)
            )
        lse = top + jnp.log(total) * LOG2E
        far = lse * 8193.0
        head = far - (far - lse)
        high.append(head)
        low.append(lse - head)
    parts = jnp.concatenate(high + low, axis=0)
    for dev in range(rows // 32):
        out_ref[dev, 128:136, :] = parts[:, dev // 4 * DH : (dev // 4 + 1) * DH]


def final_kernel(z_ref, out_ref, w_s):
    n_dev = z_ref.shape[0]
    pre = lax.axis_index("prefix")
    mine = pl.ds(pl.multiple_of(pre % 4 * 32, 32), 32)
    for c in range(2):
        lses = []
        for src in range(c, n_dev, 2):
            parts = z_ref[src, 128:136, :]
            lses.append(parts[0:4] + parts[4:8])
        top = functools.reduce(jnp.maximum, lses)
        weights = [jnp.exp2(lse - top) for lse in lses]
        scale = 1.0 / (LIFT * sum(weights))
        lines = [w * scale for w in weights]
        lines.append(jnp.zeros((DH - 2 * n_dev, DH), f32))
        w_s[c] = jnp.concatenate(lines, axis=0).T
        columns = w_s[c, mine, :]
        for i in range(HALF):
            o = 0.0
            for y, src in enumerate(range(c, n_dev, 2)):
                o = o + z_ref[src, i * 32 : (i + 1) * 32, :] * columns[:, y * 4 + i : y * 4 + i + 1]
            for g in range(GROUP):
                head = (c * HALF + i) * GROUP + g
                for s in range(2):
                    r = g * 4 + s * 2
                    out_ref[s, :, head * DH : (head + 1) * DH] = o[r : r + 2, :].astype(bf16)


def call(kernel, out_shape, ins, out_specs=VM, scratch=(), flops=0, moved=0, name=None):
    return pl.pallas_call(
        kernel,
        out_shape=out_shape,
        in_specs=ins,
        out_specs=out_specs,
        scratch_shapes=list(scratch),
        compiler_params=pltpu.CompilerParams(vmem_limit_bytes=40 * 1024 * 1024),
        cost_estimate=pl.CostEstimate(flops=flops, bytes_accessed=moved, transcendentals=0),
        name=name,
    )


def per_device(
    queries,
    prefix_keys,
    prefix_values,
    pool_keys,
    pool_values,
    new_keys,
    new_values,
    block_table,
    suffix_lengths,
):
    n_req = lax.axis_size("req")
    n_pre = lax.axis_size("prefix")
    swap = [(i, i ^ 1) for i in range(n_req)]
    core = [(i, i ^ 1) for i in range(n_pre)]
    far_keys = lax.ppermute(pool_keys, "req", swap)
    far_values = lax.ppermute(pool_values, "req", swap)
    sds = jax.ShapeDtypeStruct
    own = (queries.astype(f32) * QLIFT).astype(jnp.float16)
    own = own.reshape(4, H, DH).transpose(1, 0, 2).reshape(4 * H, DH)
    group = lax.all_gather(own, "prefix", axis=0)
    group = (group.astype(f32) * (1.0 / QLIFT)).astype(bf16)
    rows = n_pre * 32

    common = (
        group, prefix_keys, prefix_values, pool_keys, pool_values, far_keys, far_values, new_keys, new_values
    )
    part = sds((HALF, 136, rows), f32)
    cost = dict(flops=800_000_000, moved=6_000_000)
    other, meta = call(
        functools.partial(attend_kernel, True),
        (part, sds((4, 3), jnp.int32)),
        [VM] * 11,
        (VM, SM),
        name="attend_other",
        **cost,
    )(*common, suffix_lengths.reshape(-1, 128), block_table.T)
    theirs = lax.ppermute(other, "prefix", core)
    mine = call(
        functools.partial(attend_kernel, False), part, [VM] * 9 + [SM], name="attend_own", **cost
    )(*common, meta)
    merged = call(core_merge_kernel, sds((n_pre, 136, DH), f32), [VM, VM], moved=4_000_000, name="core_merge")(
        mine, theirs
    )
    spread = lax.all_to_all(merged.astype(jnp.float16), "prefix", 0, 0, tiled=True)
    return call(
        final_kernel,
        sds((2, 2, H * DH), bf16),
        [VM],
        VM,
        [pltpu.VMEM((2, DH, DH), f32)],
        moved=1_000_000,
        name="final",
    )(spread.astype(f32))


def solution(mesh):
    placed = (
        P(None, ("req", "prefix"), None),
        P("prefix", None),
        P("prefix", None),
        P(("req", "prefix"), None, None),
        P(("req", "prefix"), None, None),
        P(None, ("req", "prefix"), None),
        P(None, ("req", "prefix"), None),
        P(),
        P(),
    )
    return jax.shard_map(
        per_device,
        mesh=mesh,
        in_specs=placed,
        out_specs=P(None, ("req", "prefix"), None),
        check_vma=False,
    )
```

```python
import functools
import math

import jax
import jax.numpy as jnp
from jax import lax
from jax.experimental import pallas as pl
from jax.experimental.pallas import tpu as pltpu
from jax.sharding import PartitionSpec as P

H = 64
KVH = 8
DH = 128
BLK = 128
GROUP = H // KVH
HALF = KVH // 2
NEG = -1e30
LOG2E = 1.0 / math.log(2.0)
EXPO = LOG2E / math.sqrt(DH)
LIFT = 8192.0
QLIFT = 2048.0

bf16 = jnp.bfloat16
f32 = jnp.float32
NT = (((1,), (1,)), ((), ()))
VM = pl.BlockSpec(memory_space=pltpu.VMEM)


def find_owners(len_ref, table_ref, meta_ref):
    req = lax.axis_index("req")
    pre = lax.axis_index("prefix")
    n_pre = lax.axis_size("prefix")
    pair_rows = 4 * n_pre
    per_line = 128 // pair_rows
    pair = req // 2
    side = req % 2
    line = pair // per_line
    first = (pair % per_line) * pair_rows
    table = table_ref[:, pl.ds(pl.multiple_of(line * 128, 128), 128)]
    lane = lax.broadcasted_iota(jnp.int32, table.shape, 1) - first
    block = lax.broadcasted_iota(jnp.int32, table.shape, 0)
    left = jnp.broadcast_to(len_ref[pl.ds(line, 1), :], table.shape) - block * BLK
    usable = (left > 0) & (lane >= 0) & (lane < pair_rows)
    for n in range(4):
        holder = side if n < 2 else 1 - side
        slot = (holder * n_pre + pre) * 2 + n % 2
        hit = (table == slot) & usable
        found = jnp.sum(jnp.where(hit, lane * 256 + jnp.minimum(left, BLK), 0))
        owner = found // 256 - side * (pair_rows // 2)
        mine = (owner >= 0) & (owner < pair_rows // 2)
        owner = jnp.where(mine, owner, 0)
        meta_ref[n, 0] = owner // 2
        meta_ref[n, 1] = owner % 2
        meta_ref[n, 2] = jnp.where(mine, found % 256, 0)


def attend_kernel(
    flip, q_ref, pk_ref, pv_ref, ok_ref, ov_ref, xk_ref, xv_ref, nk_ref, nv_ref, len_ref, table_ref,
    out_ref, meta_ref,
):
    pre = lax.axis_index("prefix")
    half = pre % 2
    if flip:
        half = 1 - half
    find_owners(len_ref, table_ref, meta_ref)
    n_dev = q_ref.shape[0]
    rows = n_dev * 32
    n_quads = n_dev // 4
    n_blocks = pk_ref.shape[0] // BLK
    ones = jnp.ones((16, BLK), bf16)
    first = half * HALF

    def head_lanes(i):
        return pl.ds(pl.multiple_of((first + i) * DH, DH), DH)

    def tokens(ref, i):
        pair = [ref[s, :, head_lanes(i)].astype(f32) for s in range(2)]
        return jnp.concatenate(pair + [jnp.zeros((12, DH), f32)], axis=0).astype(bf16)

    def products(i):
        q = q_ref[:, pl.ds(pl.multiple_of((first + i) * 32, 32), 32), :].reshape(rows, DH)
        return lax.dot_general(pk_ref[:, head_lanes(i)], q, NT, preferred_element_type=f32)

    def weigh(scores):
        peaks, ws = [], []
        for b in range(n_blocks):
            s = scores[b * BLK : (b + 1) * BLK]
            peak = jnp.max(s, axis=0, keepdims=True)
            ws.append(jnp.exp2((s - peak) * EXPO).astype(bf16))
            peaks.append(peak)
        return peaks, ws

    def collect(i, ws):
        outs = []
        for b in range(n_blocks):
            v = jnp.concatenate([pv_ref[b * BLK : (b + 1) * BLK, head_lanes(i)].T, ones], axis=0)
            outs.append(jnp.dot(v, ws[b], preferred_element_type=f32)[0:136])
        return outs

    key = lax.broadcasted_iota(jnp.int32, (BLK, DH), 0)
    lane = lax.broadcasted_iota(jnp.int32, (BLK, DH), 1)
    lane_head, lane_req, lane_step = lane // 32, lane % 2, lane // 2 % 2
    own_rows = pl.ds(pl.multiple_of(first * 32, DH), DH)
    stage = []
    for n in range(5):
        if n < 4:
            kr, vr = (ok_ref, ov_ref) if n < 2 else (xk_ref, xv_ref)
            ks = [kr[n % 2, :, head_lanes(i)] for i in range(HALF)]
            vs = [vr[n % 2, :, head_lanes(i)].T for i in range(HALF)]
            dev = meta_ref[n, 0]
            live = key < jnp.where(lane_req == meta_ref[n, 1], meta_ref[n, 2], 0)
        else:
            ks = [tokens(nk_ref, i) for i in range(HALF)]
            fill = jnp.zeros((BLK - HALF * 16, DH), bf16)
            vs = [jnp.concatenate([tokens(nv_ref, i) for i in range(HALF)] + [fill], axis=0).T]
            dev = pre
            live = ((key < 4) & (key % 2 == lane_req) & (key // 2 <= lane_step))[0:16]
        count = ks[0].shape[0]
        every = lax.dot_general(
            jnp.concatenate(ks, axis=0), q_ref[dev, own_rows, :], NT, preferred_element_type=f32
        )
        stage.append((n, vs, dev, live, count, every))
    scores = [products(i) for i in range(HALF)]
    weighed = []
    for n, vs, dev, live, count, every in stage:
        s = every[0:count]
        for i in range(1, HALF):
            s = jnp.where(lane_head[0:count] == i, every[i * count : (i + 1) * count], s)
        s = jnp.where(live, s, NEG)
        peak = jnp.max(s, axis=0, keepdims=True)
        w = jnp.where(live, jnp.exp2((s - peak) * EXPO), 0.0)
        ws = [jnp.where(lane_head[0:count] == i, w, 0.0).astype(bf16) for i in range(HALF)]
        if n == 4:
            ws.append(fill)
        v = jnp.concatenate([jnp.concatenate(vs, axis=1), jnp.concatenate([ones] * len(vs), axis=1)], axis=0)
        weighed.append((dev, peak, v, ws))
    extra = []
    for dev, peak, v, ws in weighed:
        o = jnp.dot(v, jnp.concatenate(ws, axis=0), preferred_element_type=f32)[0:136]
        extra.append((dev, peak, o))

    spot = lax.broadcasted_iota(jnp.int32, (1, rows), 1) // 32
    ready = weigh(scores[0])
    for i in range(HALF):
        peaks, ws = ready
        outs = collect(i, ws)
        if i + 1 < HALF:
            ready = weigh(scores[i + 1])
        wides = []
        for dev, peak, o in extra:
            turn = (dev + (4 - i)) % 4 * 32
            moved = pltpu.roll(peak, turn, 1)
            wides.append(jnp.where(spot == dev, jnp.concatenate([moved] * n_quads, axis=1), NEG))
        top = functools.reduce(jnp.maximum, peaks + wides)
        both = 0.0
        for peak, o in zip(peaks, outs):
            both = both + jnp.exp2((peak - top) * EXPO) * o
        out_ref[i] = both
        for (dev, peak, o), wide in zip(extra, wides):
            turn = (dev + (4 - i)) % 4 * 32
            f = jnp.exp2((wide - top) * EXPO)
            f = sum(f[:, quad * DH : (quad + 1) * DH] for quad in range(n_quads))
            at = pl.ds(pl.multiple_of(dev // 4 * DH, DH), DH)
            out_ref[i, :, at] = out_ref[i, :, at] + pltpu.roll(o, turn, 1) * f
        out_ref[i, 132:136, :] = jnp.broadcast_to(top * EXPO, (4, rows))


def core_merge_kernel(a_ref, b_ref, out_ref):
    rows = a_ref.shape[2]
    high, low = [], []
    for i in range(HALF):
        pa = a_ref[i, 132:133, :]
        pb = b_ref[i, 132:133, :]
        top = jnp.maximum(pa, pb)
        wa = jnp.exp2(pa - top)
        wb = jnp.exp2(pb - top)
        total = a_ref[i, 128:129, :] * wa + b_ref[i, 128:129, :] * wb
        scale = LIFT / total
        o = a_ref[i, 0:128, :] * (wa * scale) + b_ref[i, 0:128, :] * (wb * scale)
        for quad in range(rows // DH):
            out_ref[quad * 4 : quad * 4 + 4, i * 32 : (i + 1) * 32, :] = (
                o[:, quad * DH : (quad + 1) * DH].T.reshape(4, 32, DH)
            )
        lse = top + jnp.log(total) * LOG2E
        far = lse * 8193.0
        head = far - (far - lse)
        high.append(head)
        low.append(lse - head)
    parts = jnp.concatenate(high + low, axis=0)
    for dev in range(rows // 32):
        out_ref[dev, 128:136, :] = parts[:, dev // 4 * DH : (dev // 4 + 1) * DH]


def final_kernel(z_ref, out_ref, w_s):
    n_dev = z_ref.shape[0]
    pre = lax.axis_index("prefix")
    mine = pl.ds(pl.multiple_of(pre % 4 * 32, 32), 32)
    for c in range(2):
        lses = []
        for src in range(c, n_dev, 2):
            parts = z_ref[src, 128:136, :]
            lses.append(parts[0:4] + parts[4:8])
        top = functools.reduce(jnp.maximum, lses)
        weights = [jnp.exp2(lse - top) for lse in lses]
        scale = 1.0 / (LIFT * sum(weights))
        lines = [w * scale for w in weights]
        lines.append(jnp.zeros((DH - 2 * n_dev, DH), f32))
        w_s[c] = jnp.concatenate(lines, axis=0).T
        columns = w_s[c, mine, :]
        for i in range(HALF):
            o = 0.0
            for y, src in enumerate(range(c, n_dev, 2)):
                o = o + z_ref[src, i * 32 : (i + 1) * 32, :] * columns[:, y * 4 + i : y * 4 + i + 1]
            for g in range(GROUP):
                head = (c * HALF + i) * GROUP + g
                for s in range(2):
                    r = g * 4 + s * 2
                    out_ref[s, :, head * DH : (head + 1) * DH] = o[r : r + 2, :].astype(bf16)


def call(kernel, out_shape, ins, out_specs=VM, scratch=(), flops=0, moved=0, name=None):
    return pl.pallas_call(
        kernel,
        out_shape=out_shape,
        in_specs=ins,
        out_specs=out_specs,
        scratch_shapes=list(scratch),
        compiler_params=pltpu.CompilerParams(vmem_limit_bytes=40 * 1024 * 1024),
        cost_estimate=pl.CostEstimate(flops=flops, bytes_accessed=moved, transcendentals=0),
        name=name,
    )


def per_device(
    queries,
    prefix_keys,
    prefix_values,
    pool_keys,
    pool_values,
    new_keys,
    new_values,
    block_table,
    suffix_lengths,
):
    n_req = lax.axis_size("req")
    n_pre = lax.axis_size("prefix")
    swap = [(i, i ^ 1) for i in range(n_req)]
    core = [(i, i ^ 1) for i in range(n_pre)]
    far_keys = lax.ppermute(pool_keys, "req", swap)
    far_values = lax.ppermute(pool_values, "req", swap)
    sds = jax.ShapeDtypeStruct
    own = (queries.astype(f32) * QLIFT).astype(jnp.float16)
    own = own.reshape(4, H, DH).transpose(1, 0, 2).reshape(4 * H, DH)
    group = lax.all_gather(own, "prefix", axis=0)
    group = (group.astype(f32) * (1.0 / QLIFT)).astype(bf16)
    rows = n_pre * 32


    def attend(flip):
        return call(
            functools.partial(attend_kernel, flip),
            sds((HALF, 136, rows), f32),
            [VM] * 11,
            VM,
            [pltpu.SMEM((4, 3), jnp.int32)],
            flops=800_000_000,
            moved=6_000_000,
            name="attend_other" if flip else "attend_own",
        )(
            group, prefix_keys, prefix_values, pool_keys, pool_values, far_keys, far_values,
            new_keys, new_values, suffix_lengths.reshape(-1, 128), block_table.T,
        )

    theirs = lax.ppermute(attend(True), "prefix", core)
    mine = attend(False)
    merged = call(core_merge_kernel, sds((n_pre, 136, DH), f32), [VM, VM], moved=4_000_000, name="core_merge")(
        mine, theirs
    )
    spread = lax.all_to_all(merged.astype(jnp.float16), "prefix", 0, 0, tiled=True)
    return call(
        final_kernel,
        sds((2, 2, H * DH), bf16),
        [VM],
        VM,
        [pltpu.VMEM((2, DH, DH), f32)],
        moved=1_000_000,
        name="final",
    )(spread.astype(f32))


def solution(mesh):
    placed = (
        P(None, ("req", "prefix"), None),
        P("prefix", None),
        P("prefix", None),
        P(("req", "prefix"), None, None),
        P(("req", "prefix"), None, None),
        P(None, ("req", "prefix"), None),
        P(None, ("req", "prefix"), None),
        P(),
        P(),
    )
    return jax.shard_map(
        per_device,
        mesh=mesh,
        in_specs=placed,
        out_specs=P(None, ("req", "prefix"), None),
        check_vma=False,
    )
```

```python
import functools
import math

import jax
import jax.numpy as jnp
from jax import lax
from jax.experimental import pallas as pl
from jax.experimental.pallas import tpu as pltpu
from jax.sharding import PartitionSpec as P

H = 64
KVH = 8
DH = 128
BLK = 128
GROUP = H // KVH
HALF = KVH // 2
NEG = -1e30
LOG2E = 1.0 / math.log(2.0)
EXPO = LOG2E / math.sqrt(DH)
LIFT = 8192.0
QLIFT = 2048.0

bf16 = jnp.bfloat16
f32 = jnp.float32
NT = (((1,), (1,)), ((), ()))
VM = pl.BlockSpec(memory_space=pltpu.VMEM)


def find_owners(len_ref, table_ref, meta_ref):
    req = lax.axis_index("req")
    pre = lax.axis_index("prefix")
    n_pre = lax.axis_size("prefix")
    pair_rows = 4 * n_pre
    per_line = 128 // pair_rows
    pair = req // 2
    side = req % 2
    line = pair // per_line
    first = (pair % per_line) * pair_rows
    table = table_ref[:, pl.ds(pl.multiple_of(line * 128, 128), 128)]
    lane = lax.broadcasted_iota(jnp.int32, table.shape, 1) - first
    block = lax.broadcasted_iota(jnp.int32, table.shape, 0)
    left = jnp.broadcast_to(len_ref[pl.ds(line, 1), :], table.shape) - block * BLK
    usable = (left > 0) & (lane >= 0) & (lane < pair_rows)
    for n in range(4):
        holder = side if n < 2 else 1 - side
        slot = (holder * n_pre + pre) * 2 + n % 2
        hit = (table == slot) & usable
        found = jnp.sum(jnp.where(hit, lane * 256 + jnp.minimum(left, BLK), 0))
        owner = found // 256 - side * (pair_rows // 2)
        mine = (owner >= 0) & (owner < pair_rows // 2)
        owner = jnp.where(mine, owner, 0)
        meta_ref[n, 0] = owner // 2
        meta_ref[n, 1] = owner % 2
        meta_ref[n, 2] = jnp.where(mine, found % 256, 0)


def attend_kernel(
    flip, q_ref, pk_ref, pv_ref, own_ref, far_ref, nk_ref, nv_ref, len_ref, table_ref,
    out_ref, meta_ref,
):
    pre = lax.axis_index("prefix")
    half = pre % 2
    if flip:
        half = 1 - half
    find_owners(len_ref, table_ref, meta_ref)
    n_dev = q_ref.shape[0]
    rows = n_dev * 32
    n_quads = n_dev // 4
    n_blocks = pk_ref.shape[0] // BLK
    ones = jnp.ones((16, BLK), bf16)
    first = half * HALF

    def head_lanes(i):
        return pl.ds(pl.multiple_of((first + i) * DH, DH), DH)

    def tokens(ref, i):
        pair = [ref[s, :, head_lanes(i)].astype(f32) for s in range(2)]
        return jnp.concatenate(pair + [jnp.zeros((12, DH), f32)], axis=0).astype(bf16)

    def products(i):
        q = q_ref[:, pl.ds(pl.multiple_of((first + i) * 32, 32), 32), :].reshape(rows, DH)
        return lax.dot_general(pk_ref[:, head_lanes(i)], q, NT, preferred_element_type=f32)

    def weigh(scores):
        peaks, ws = [], []
        for b in range(n_blocks):
            s = scores[b * BLK : (b + 1) * BLK]
            peak = jnp.max(s, axis=0, keepdims=True)
            ws.append(jnp.exp2((s - peak) * EXPO).astype(bf16))
            peaks.append(peak)
        return peaks, ws

    def collect(i, ws):
        outs = []
        for b in range(n_blocks):
            v = jnp.concatenate([pv_ref[b * BLK : (b + 1) * BLK, head_lanes(i)].T, ones], axis=0)
            outs.append(jnp.dot(v, ws[b], preferred_element_type=f32)[0:136])
        return outs

    key = lax.broadcasted_iota(jnp.int32, (BLK, DH), 0)
    lane = lax.broadcasted_iota(jnp.int32, (BLK, DH), 1)
    lane_head, lane_req, lane_step = lane // 32, lane % 2, lane // 2 % 2
    own_rows = pl.ds(pl.multiple_of(first * 32, DH), DH)
    stage = []
    for n in range(5):
        if n < 4:
            pool = own_ref if n < 2 else far_ref
            ks = [pool[0, n % 2, :, head_lanes(i)] for i in range(HALF)]
            vs = [pool[1, n % 2, :, head_lanes(i)].T for i in range(HALF)]
            dev = meta_ref[n, 0]
            live = key < jnp.where(lane_req == meta_ref[n, 1], meta_ref[n, 2], 0)
        else:
            ks = [tokens(nk_ref, i) for i in range(HALF)]
            fill = jnp.zeros((BLK - HALF * 16, DH), bf16)
            vs = [jnp.concatenate([tokens(nv_ref, i) for i in range(HALF)] + [fill], axis=0).T]
            dev = pre
            live = ((key < 4) & (key % 2 == lane_req) & (key // 2 <= lane_step))[0:16]
        count = ks[0].shape[0]
        every = lax.dot_general(
            jnp.concatenate(ks, axis=0), q_ref[dev, own_rows, :], NT, preferred_element_type=f32
        )
        stage.append((n, vs, dev, live, count, every))
    scores = [products(i) for i in range(HALF)]
    weighed = []
    for n, vs, dev, live, count, every in stage:
        s = every[0:count]
        for i in range(1, HALF):
            s = jnp.where(lane_head[0:count] == i, every[i * count : (i + 1) * count], s)
        s = jnp.where(live, s, NEG)
        peak = jnp.max(s, axis=0, keepdims=True)
        w = jnp.where(live, jnp.exp2((s - peak) * EXPO), 0.0)
        ws = [jnp.where(lane_head[0:count] == i, w, 0.0).astype(bf16) for i in range(HALF)]
        if n == 4:
            ws.append(fill)
        v = jnp.concatenate([jnp.concatenate(vs, axis=1), jnp.concatenate([ones] * len(vs), axis=1)], axis=0)
        weighed.append((dev, peak, v, ws))
    extra = []
    for dev, peak, v, ws in weighed:
        o = jnp.dot(v, jnp.concatenate(ws, axis=0), preferred_element_type=f32)[0:136]
        extra.append((dev, peak, o))

    spot = lax.broadcasted_iota(jnp.int32, (1, rows), 1) // 32
    ready = weigh(scores[0])
    for i in range(HALF):
        peaks, ws = ready
        outs = collect(i, ws)
        if i + 1 < HALF:
            ready = weigh(scores[i + 1])
        wides = []
        for dev, peak, o in extra:
            turn = (dev + (4 - i)) % 4 * 32
            moved = pltpu.roll(peak, turn, 1)
            wides.append(jnp.where(spot == dev, jnp.concatenate([moved] * n_quads, axis=1), NEG))
        top = functools.reduce(jnp.maximum, peaks + wides)
        both = 0.0
        for peak, o in zip(peaks, outs):
            both = both + jnp.exp2((peak - top) * EXPO) * o
        out_ref[i] = both
        for (dev, peak, o), wide in zip(extra, wides):
            turn = (dev + (4 - i)) % 4 * 32
            f = jnp.exp2((wide - top) * EXPO)
            f = sum(f[:, quad * DH : (quad + 1) * DH] for quad in range(n_quads))
            at = pl.ds(pl.multiple_of(dev // 4 * DH, DH), DH)
            out_ref[i, :, at] = out_ref[i, :, at] + pltpu.roll(o, turn, 1) * f
        out_ref[i, 132:136, :] = jnp.broadcast_to(top * EXPO, (4, rows))


def core_merge_kernel(a_ref, b_ref, out_ref):
    rows = a_ref.shape[2]
    high, low = [], []
    for i in range(HALF):
        pa = a_ref[i, 132:133, :]
        pb = b_ref[i, 132:133, :]
        top = jnp.maximum(pa, pb)
        wa = jnp.exp2(pa - top)
        wb = jnp.exp2(pb - top)
        total = a_ref[i, 128:129, :] * wa + b_ref[i, 128:129, :] * wb
        scale = LIFT / total
        o = a_ref[i, 0:128, :] * (wa * scale) + b_ref[i, 0:128, :] * (wb * scale)
        for quad in range(rows // DH):
            out_ref[quad * 4 : quad * 4 + 4, i * 32 : (i + 1) * 32, :] = (
                o[:, quad * DH : (quad + 1) * DH].T.reshape(4, 32, DH)
            )
        lse = top + jnp.log(total) * LOG2E
        far = lse * 8193.0
        head = far - (far - lse)
        high.append(head)
        low.append(lse - head)
    parts = jnp.concatenate(high + low, axis=0)
    for dev in range(rows // 32):
        out_ref[dev, 128:136, :] = parts[:, dev // 4 * DH : (dev // 4 + 1) * DH]


def final_kernel(z_ref, out_ref, w_s):
    n_dev = z_ref.shape[0]
    pre = lax.axis_index("prefix")
    mine = pl.ds(pl.multiple_of(pre % 4 * 32, 32), 32)
    for c in range(2):
        lses = []
        for src in range(c, n_dev, 2):
            parts = z_ref[src, 128:136, :]
            lses.append(parts[0:4] + parts[4:8])
        top = functools.reduce(jnp.maximum, lses)
        weights = [jnp.exp2(lse - top) for lse in lses]
        scale = 1.0 / (LIFT * sum(weights))
        lines = [w * scale for w in weights]
        lines.append(jnp.zeros((DH - 2 * n_dev, DH), f32))
        w_s[c] = jnp.concatenate(lines, axis=0).T
        columns = w_s[c, mine, :]
        for i in range(HALF):
            o = 0.0
            for y, src in enumerate(range(c, n_dev, 2)):
                o = o + z_ref[src, i * 32 : (i + 1) * 32, :] * columns[:, y * 4 + i : y * 4 + i + 1]
            for g in range(GROUP):
                head = (c * HALF + i) * GROUP + g
                for s in range(2):
                    r = g * 4 + s * 2
                    out_ref[s, :, head * DH : (head + 1) * DH] = o[r : r + 2, :].astype(bf16)


def call(kernel, out_shape, ins, out_specs=VM, scratch=(), flops=0, moved=0, name=None):
    return pl.pallas_call(
        kernel,
        out_shape=out_shape,
        in_specs=ins,
        out_specs=out_specs,
        scratch_shapes=list(scratch),
        compiler_params=pltpu.CompilerParams(vmem_limit_bytes=40 * 1024 * 1024),
        cost_estimate=pl.CostEstimate(flops=flops, bytes_accessed=moved, transcendentals=0),
        name=name,
    )


def per_device(
    queries,
    prefix_keys,
    prefix_values,
    pool_keys,
    pool_values,
    new_keys,
    new_values,
    block_table,
    suffix_lengths,
):
    n_req = lax.axis_size("req")
    n_pre = lax.axis_size("prefix")
    swap = [(i, i ^ 1) for i in range(n_req)]
    core = [(i, i ^ 1) for i in range(n_pre)]
    pool = jnp.stack([pool_keys, pool_values])
    far = lax.ppermute(pool, "req", swap)
    sds = jax.ShapeDtypeStruct
    own = (queries.astype(f32) * QLIFT).astype(jnp.float16)
    own = own.reshape(4, H, DH).transpose(1, 0, 2).reshape(4 * H, DH)
    group = lax.all_gather(own, "prefix", axis=0)
    group = (group.astype(f32) * (1.0 / QLIFT)).astype(bf16)
    rows = n_pre * 32


    def attend(flip):
        return call(
            functools.partial(attend_kernel, flip),
            sds((HALF, 136, rows), f32),
            [VM] * 9,
            VM,
            [pltpu.SMEM((4, 3), jnp.int32)],
            flops=800_000_000,
            moved=6_000_000,
            name="attend_other" if flip else "attend_own",
        )(
            group, prefix_keys, prefix_values, pool, far, new_keys, new_values,
            suffix_lengths.reshape(-1, 128), block_table.T,
        )

    theirs = lax.ppermute(attend(True), "prefix", core)
    mine = attend(False)
    merged = call(core_merge_kernel, sds((n_pre, 136, DH), f32), [VM, VM], moved=4_000_000, name="core_merge")(
        mine, theirs
    )
    spread = lax.all_to_all(merged.astype(jnp.float16), "prefix", 0, 0, tiled=True)
    return call(
        final_kernel,
        sds((2, 2, H * DH), bf16),
        [VM],
        VM,
        [pltpu.VMEM((2, DH, DH), f32)],
        moved=1_000_000,
        name="final",
    )(spread.astype(f32))


def solution(mesh):
    placed = (
        P(None, ("req", "prefix"), None),
        P("prefix", None),
        P("prefix", None),
        P(("req", "prefix"), None, None),
        P(("req", "prefix"), None, None),
        P(None, ("req", "prefix"), None),
        P(None, ("req", "prefix"), None),
        P(),
        P(),
    )
    return jax.shard_map(
        per_device,
        mesh=mesh,
        in_specs=placed,
        out_specs=P(None, ("req", "prefix"), None),
        check_vma=False,
    )
```

```python
import functools
import math

import jax
import jax.numpy as jnp
from jax import lax
from jax.experimental import pallas as pl
from jax.experimental.pallas import tpu as pltpu
from jax.sharding import PartitionSpec as P

H = 64
KVH = 8
DH = 128
BLK = 128
GROUP = H // KVH
HALF = KVH // 2
NEG = -1e30
LOG2E = 1.0 / math.log(2.0)
EXPO = LOG2E / math.sqrt(DH)
LIFT = 8192.0
QLIFT = 2048.0

bf16 = jnp.bfloat16
f32 = jnp.float32
NT = (((1,), (1,)), ((), ()))
VM = pl.BlockSpec(memory_space=pltpu.VMEM)


def find_owners(homes, len_ref, table_ref, meta_ref):
    req = lax.axis_index("req")
    n_pre = lax.axis_size("prefix")
    pair_rows = 4 * n_pre
    per_line = 128 // pair_rows
    pair = req // 2
    side = req % 2
    line = pair // per_line
    first = (pair % per_line) * pair_rows
    table = table_ref[:, pl.ds(pl.multiple_of(line * 128, 128), 128)]
    lane = lax.broadcasted_iota(jnp.int32, table.shape, 1) - first
    block = lax.broadcasted_iota(jnp.int32, table.shape, 0)
    left = jnp.broadcast_to(len_ref[pl.ds(line, 1), :], table.shape) - block * BLK
    usable = (left > 0) & (lane >= 0) & (lane < pair_rows)
    for n in range(2 * len(homes)):
        near, pre = homes[n // 2]
        holder = side if near else 1 - side
        slot = (holder * n_pre + pre) * 2 + n % 2
        hit = (table == slot) & usable
        found = jnp.sum(jnp.where(hit, lane * 256 + jnp.minimum(left, BLK), 0))
        owner = found // 256 - side * (pair_rows // 2)
        mine = (owner >= 0) & (owner < pair_rows // 2)
        owner = jnp.where(mine, owner, 0)
        meta_ref[n, 0] = owner // 2
        meta_ref[n, 1] = owner % 2
        meta_ref[n, 2] = jnp.where(mine, found % 256, 0)


def attend_kernel(
    flip, q_ref, pk_ref, pv_ref, nk_ref, nv_ref, len_ref, table_ref, *refs
):
    pre = lax.axis_index("prefix")
    half = pre % 2
    if flip:
        half = 1 - half
    *pools, out_ref, meta_ref = refs
    homes = [(True, pre), (False, pre), (False, pre + 1 - 2 * (pre % 2))][0 : len(pools)]
    find_owners(homes, len_ref, table_ref, meta_ref)
    n_slots = 2 * len(pools)
    n_dev = q_ref.shape[0]
    rows = n_dev * 32
    n_quads = n_dev // 4
    n_blocks = pk_ref.shape[0] // BLK
    ones = jnp.ones((16, BLK), bf16)
    first = half * HALF

    def head_lanes(i):
        return pl.ds(pl.multiple_of((first + i) * DH, DH), DH)

    def tokens(ref, i):
        pair = [ref[s, :, head_lanes(i)].astype(f32) for s in range(2)]
        return jnp.concatenate(pair + [jnp.zeros((12, DH), f32)], axis=0).astype(bf16)

    def products(i):
        q = q_ref[:, pl.ds(pl.multiple_of((first + i) * 32, 32), 32), :].reshape(rows, DH)
        return lax.dot_general(pk_ref[:, head_lanes(i)], q, NT, preferred_element_type=f32)

    def weigh(scores):
        peaks, ws = [], []
        for b in range(n_blocks):
            s = scores[b * BLK : (b + 1) * BLK]
            peak = jnp.max(s, axis=0, keepdims=True)
            ws.append(jnp.exp2((s - peak) * EXPO).astype(bf16))
            peaks.append(peak)
        return peaks, ws

    def collect(i, ws):
        outs = []
        for b in range(n_blocks):
            v = jnp.concatenate([pv_ref[b * BLK : (b + 1) * BLK, head_lanes(i)].T, ones], axis=0)
            outs.append(jnp.dot(v, ws[b], preferred_element_type=f32)[0:136])
        return outs

    key = lax.broadcasted_iota(jnp.int32, (BLK, DH), 0)
    lane = lax.broadcasted_iota(jnp.int32, (BLK, DH), 1)
    lane_head, lane_req, lane_step = lane // 32, lane % 2, lane // 2 % 2
    own_rows = pl.ds(pl.multiple_of(first * 32, DH), DH)
    stage = []
    for n in range(n_slots + 1):
        if n < n_slots:
            pool = pools[n // 2]
            ks = [pool[0, n % 2, :, i * DH : (i + 1) * DH] for i in range(HALF)]
            vs = [pool[1, n % 2, :, i * DH : (i + 1) * DH].T for i in range(HALF)]
            dev = meta_ref[n, 0]
            live = key < jnp.where(lane_req == meta_ref[n, 1], meta_ref[n, 2], 0)
        else:
            ks = [tokens(nk_ref, i) for i in range(HALF)]
            fill = jnp.zeros((BLK - HALF * 16, DH), bf16)
            vs = [jnp.concatenate([tokens(nv_ref, i) for i in range(HALF)] + [fill], axis=0).T]
            dev = pre
            live = ((key < 4) & (key % 2 == lane_req) & (key // 2 <= lane_step))[0:16]
        count = ks[0].shape[0]
        every = lax.dot_general(
            jnp.concatenate(ks, axis=0), q_ref[dev, own_rows, :], NT, preferred_element_type=f32
        )
        stage.append((n, vs, dev, live, count, every))
    scores = [products(i) for i in range(HALF)]
    weighed = []
    for n, vs, dev, live, count, every in stage:
        s = every[0:count]
        for i in range(1, HALF):
            s = jnp.where(lane_head[0:count] == i, every[i * count : (i + 1) * count], s)
        s = jnp.where(live, s, NEG)
        peak = jnp.max(s, axis=0, keepdims=True)
        w = jnp.where(live, jnp.exp2((s - peak) * EXPO), 0.0)
        ws = [jnp.where(lane_head[0:count] == i, w, 0.0).astype(bf16) for i in range(HALF)]
        if n == n_slots:
            ws.append(fill)
        v = jnp.concatenate([jnp.concatenate(vs, axis=1), jnp.concatenate([ones] * len(vs), axis=1)], axis=0)
        weighed.append((dev, peak, v, ws))
    extra = []
    for dev, peak, v, ws in weighed:
        o = jnp.dot(v, jnp.concatenate(ws, axis=0), preferred_element_type=f32)[0:136]
        extra.append((dev, peak, o))

    spot = lax.broadcasted_iota(jnp.int32, (1, rows), 1) // 32
    ready = weigh(scores[0])
    for i in range(HALF):
        peaks, ws = ready
        outs = collect(i, ws)
        if i + 1 < HALF:
            ready = weigh(scores[i + 1])
        wides = []
        for dev, peak, o in extra:
            turn = (dev + (4 - i)) % 4 * 32
            moved = pltpu.roll(peak, turn, 1)
            wides.append(jnp.where(spot == dev, jnp.concatenate([moved] * n_quads, axis=1), NEG))
        top = functools.reduce(jnp.maximum, peaks + wides)
        both = 0.0
        for peak, o in zip(peaks, outs):
            both = both + jnp.exp2((peak - top) * EXPO) * o
        out_ref[i] = both
        for (dev, peak, o), wide in zip(extra, wides):
            turn = (dev + (4 - i)) % 4 * 32
            f = jnp.exp2((wide - top) * EXPO)
            f = sum(f[:, quad * DH : (quad + 1) * DH] for quad in range(n_quads))
            at = pl.ds(pl.multiple_of(dev // 4 * DH, DH), DH)
            out_ref[i, :, at] = out_ref[i, :, at] + pltpu.roll(o, turn, 1) * f
        out_ref[i, 132:136, :] = jnp.broadcast_to(top * EXPO, (4, rows))


def core_merge_kernel(a_ref, b_ref, out_ref):
    rows = a_ref.shape[2]
    high, low = [], []
    for i in range(HALF):
        pa = a_ref[i, 132:133, :]
        pb = b_ref[i, 132:133, :]
        top = jnp.maximum(pa, pb)
        wa = jnp.exp2(pa - top)
        wb = jnp.exp2(pb - top)
        total = a_ref[i, 128:129, :] * wa + b_ref[i, 128:129, :] * wb
        scale = LIFT / total
        o = a_ref[i, 0:128, :] * (wa * scale) + b_ref[i, 0:128, :] * (wb * scale)
        for quad in range(rows // DH):
            out_ref[quad * 4 : quad * 4 + 4, i * 32 : (i + 1) * 32, :] = (
                o[:, quad * DH : (quad + 1) * DH].T.reshape(4, 32, DH)
            )
        lse = top + jnp.log(total) * LOG2E
        far = lse * 8193.0
        head = far - (far - lse)
        high.append(head)
        low.append(lse - head)
    parts = jnp.concatenate(high + low, axis=0)
    for dev in range(rows // 32):
        out_ref[dev, 128:136, :] = parts[:, dev // 4 * DH : (dev // 4 + 1) * DH]


def final_kernel(z_ref, out_ref, w_s):
    n_dev = z_ref.shape[0]
    pre = lax.axis_index("prefix")
    mine = pl.ds(pl.multiple_of(pre % 4 * 32, 32), 32)
    for c in range(2):
        lses = []
        for src in range(c, n_dev, 2):
            parts = z_ref[src, 128:136, :]
            lses.append(parts[0:4] + parts[4:8])
        top = functools.reduce(jnp.maximum, lses)
        weights = [jnp.exp2(lse - top) for lse in lses]
        scale = 1.0 / (LIFT * sum(weights))
        lines = [w * scale for w in weights]
        lines.append(jnp.zeros((DH - 2 * n_dev, DH), f32))
        w_s[c] = jnp.concatenate(lines, axis=0).T
        columns = w_s[c, mine, :]
        for i in range(HALF):
            o = 0.0
            for y, src in enumerate(range(c, n_dev, 2)):
                o = o + z_ref[src, i * 32 : (i + 1) * 32, :] * columns[:, y * 4 + i : y * 4 + i + 1]
            for g in range(GROUP):
                head = (c * HALF + i) * GROUP + g
                for s in range(2):
                    r = g * 4 + s * 2
                    out_ref[s, :, head * DH : (head + 1) * DH] = o[r : r + 2, :].astype(bf16)


def call(kernel, out_shape, ins, out_specs=VM, scratch=(), flops=0, moved=0, name=None):
    return pl.pallas_call(
        kernel,
        out_shape=out_shape,
        in_specs=ins,
        out_specs=out_specs,
        scratch_shapes=list(scratch),
        compiler_params=pltpu.CompilerParams(vmem_limit_bytes=40 * 1024 * 1024),
        cost_estimate=pl.CostEstimate(flops=flops, bytes_accessed=moved, transcendentals=0),
        name=name,
    )


def per_device(
    queries,
    prefix_keys,
    prefix_values,
    pool_keys,
    pool_values,
    new_keys,
    new_values,
    block_table,
    suffix_lengths,
):
    n_req = lax.axis_size("req")
    n_pre = lax.axis_size("prefix")
    swap = [(i, i ^ 1) for i in range(n_req)]
    core = [(i, i ^ 1) for i in range(n_pre)]
    across = [(i, (i ^ 1) ^ n_pre) for i in range(n_req * n_pre)]
    pool = jnp.stack([pool_keys, pool_values])
    wide = HALF * DH
    side = lax.axis_index("prefix") % 2
    pool_same = lax.dynamic_slice_in_dim(pool, side * wide, wide, 3)
    pool_cross = lax.dynamic_slice_in_dim(pool, (1 - side) * wide, wide, 3)
    pool_same, pool_cross, queries = lax.optimization_barrier((pool_same, pool_cross, queries))
    far_same = lax.ppermute(pool_same, "req", swap)
    far_cross = lax.ppermute(pool_cross, ("req", "prefix"), across)
    sds = jax.ShapeDtypeStruct
    own = (queries.astype(f32) * QLIFT).astype(jnp.float16)
    own = own.reshape(4, H, DH).transpose(1, 0, 2).reshape(4 * H, DH)
    group = lax.all_gather(own, "prefix", axis=0)
    group = (group.astype(f32) * (1.0 / QLIFT)).astype(bf16)
    rows = n_pre * 32


    def attend(flip, pools):
        return call(
            functools.partial(attend_kernel, flip),
            sds((HALF, 136, rows), f32),
            [VM] * (7 + len(pools)),
            VM,
            [pltpu.SMEM((2 * len(pools), 3), jnp.int32)],
            flops=800_000_000,
            moved=6_000_000,
            name="attend_other" if flip else "attend_own",
        )(
            group, prefix_keys, prefix_values, new_keys, new_values,
            suffix_lengths.reshape(-1, 128), block_table.T, *pools,
        )

    other, far_same, far_cross = lax.optimization_barrier((attend(True, [pool_cross]), far_same, far_cross))
    theirs = lax.ppermute(other, "prefix", core)
    mine = attend(False, [pool_same, far_same, far_cross])
    merged = call(core_merge_kernel, sds((n_pre, 136, DH), f32), [VM, VM], moved=4_000_000, name="core_merge")(
        mine, theirs
    )
    spread = lax.all_to_all(merged.astype(jnp.float16), "prefix", 0, 0, tiled=True)
    return call(
        final_kernel,
        sds((2, 2, H * DH), bf16),
        [VM],
        VM,
        [pltpu.VMEM((2, DH, DH), f32)],
        moved=1_000_000,
        name="final",
    )(spread.astype(f32))


def solution(mesh):
    placed = (
        P(None, ("req", "prefix"), None),
        P("prefix", None),
        P("prefix", None),
        P(("req", "prefix"), None, None),
        P(("req", "prefix"), None, None),
        P(None, ("req", "prefix"), None),
        P(None, ("req", "prefix"), None),
        P(),
        P(),
    )
    return jax.shard_map(
        per_device,
        mesh=mesh,
        in_specs=placed,
        out_specs=P(None, ("req", "prefix"), None),
        check_vma=False,
    )
```

```python
import functools
import math

import jax
import jax.numpy as jnp
from jax import lax
from jax.experimental import pallas as pl
from jax.experimental.pallas import tpu as pltpu
from jax.sharding import PartitionSpec as P

H = 64
KVH = 8
DH = 128
BLK = 128
GROUP = H // KVH
HALF = KVH // 2
NEG = -1e30
LOG2E = 1.0 / math.log(2.0)
EXPO = LOG2E / math.sqrt(DH)
LIFT = 8192.0
QLIFT = 2048.0

bf16 = jnp.bfloat16
f32 = jnp.float32
NT = (((1,), (1,)), ((), ()))
VM = pl.BlockSpec(memory_space=pltpu.VMEM)


def find_owners(homes, len_ref, table_ref, meta_ref):
    req = lax.axis_index("req")
    n_pre = lax.axis_size("prefix")
    pair_rows = 4 * n_pre
    per_line = 128 // pair_rows
    pair = req // 2
    side = req % 2
    line = pair // per_line
    first = (pair % per_line) * pair_rows
    table = table_ref[:, pl.ds(pl.multiple_of(line * 128, 128), 128)]
    lane = lax.broadcasted_iota(jnp.int32, table.shape, 1) - first
    block = lax.broadcasted_iota(jnp.int32, table.shape, 0)
    left = jnp.broadcast_to(len_ref[pl.ds(line, 1), :], table.shape) - block * BLK
    usable = (left > 0) & (lane >= 0) & (lane < pair_rows)
    for n in range(2 * len(homes)):
        near, pre = homes[n // 2]
        holder = side if near else 1 - side
        slot = (holder * n_pre + pre) * 2 + n % 2
        hit = (table == slot) & usable
        found = jnp.sum(jnp.where(hit, lane * 256 + jnp.minimum(left, BLK), 0))
        owner = found // 256 - side * (pair_rows // 2)
        mine = (owner >= 0) & (owner < pair_rows // 2)
        owner = jnp.where(mine, owner, 0)
        meta_ref[n, 0] = owner // 2
        meta_ref[n, 1] = owner % 2
        meta_ref[n, 2] = jnp.where(mine, found % 256, 0)


def attend_kernel(
    flip, q_ref, pk_ref, pv_ref, nk_ref, nv_ref, len_ref, table_ref, *refs
):
    pre = lax.axis_index("prefix")
    half = pre % 2
    if flip:
        half = 1 - half
    *pools, out_ref, meta_ref = refs
    homes = [(True, pre), (False, pre), (False, pre + 1 - 2 * (pre % 2))][0 : len(pools)]
    find_owners(homes, len_ref, table_ref, meta_ref)
    n_slots = 2 * len(pools)
    n_dev = q_ref.shape[0]
    rows = n_dev * 32
    n_quads = n_dev // 4
    n_blocks = pk_ref.shape[0] // BLK
    ones = jnp.ones((16, BLK), bf16)
    first = half * HALF

    def head_lanes(i):
        return pl.ds(pl.multiple_of((first + i) * DH, DH), DH)

    def tokens(ref, i):
        pair = [ref[s, :, head_lanes(i)].astype(f32) for s in range(2)]
        return jnp.concatenate(pair + [jnp.zeros((12, DH), f32)], axis=0).astype(bf16)

    def products(i):
        q = q_ref[:, pl.ds(pl.multiple_of((first + i) * 32, 32), 32), :].reshape(rows, DH)
        return lax.dot_general(pk_ref[:, head_lanes(i)], q, NT, preferred_element_type=f32)

    def weigh(scores):
        peaks, ws = [], []
        for b in range(n_blocks):
            s = scores[b * BLK : (b + 1) * BLK]
            peak = jnp.max(s, axis=0, keepdims=True)
            ws.append(jnp.exp2((s - peak) * EXPO).astype(bf16))
            peaks.append(peak)
        return peaks, ws

    def collect(i, ws):
        outs = []
        for b in range(n_blocks):
            v = jnp.concatenate([pv_ref[b * BLK : (b + 1) * BLK, head_lanes(i)].T, ones], axis=0)
            outs.append(jnp.dot(v, ws[b], preferred_element_type=f32)[0:136])
        return outs

    key = lax.broadcasted_iota(jnp.int32, (BLK, DH), 0)
    lane = lax.broadcasted_iota(jnp.int32, (BLK, DH), 1)
    lane_head, lane_req, lane_step = lane // 32, lane % 2, lane // 2 % 2
    own_rows = pl.ds(pl.multiple_of(first * 32, DH), DH)
    stage = []
    for n in range(n_slots + 1):
        if n < n_slots:
            pool = pools[n // 2]
            ks = [pool[0, n % 2, :, i * DH : (i + 1) * DH] for i in range(HALF)]
            vs = [pool[1, n % 2, :, i * DH : (i + 1) * DH].T for i in range(HALF)]
            dev = meta_ref[n, 0]
            live = key < jnp.where(lane_req == meta_ref[n, 1], meta_ref[n, 2], 0)
        else:
            ks = [tokens(nk_ref, i) for i in range(HALF)]
            fill = jnp.zeros((BLK - HALF * 16, DH), bf16)
            vs = [jnp.concatenate([tokens(nv_ref, i) for i in range(HALF)] + [fill], axis=0).T]
            dev = pre
            live = ((key < 4) & (key % 2 == lane_req) & (key // 2 <= lane_step))[0:16]
        count = ks[0].shape[0]
        every = lax.dot_general(
            jnp.concatenate(ks, axis=0), q_ref[dev, own_rows, :], NT, preferred_element_type=f32
        )
        stage.append((n, vs, dev, live, count, every))
    scores = [products(i) for i in range(HALF)]
    weighed = []
    for n, vs, dev, live, count, every in stage:
        s = every[0:count]
        for i in range(1, HALF):
            s = jnp.where(lane_head[0:count] == i, every[i * count : (i + 1) * count], s)
        s = jnp.where(live, s, NEG)
        peak = jnp.max(s, axis=0, keepdims=True)
        w = jnp.where(live, jnp.exp2((s - peak) * EXPO), 0.0)
        ws = [jnp.where(lane_head[0:count] == i, w, 0.0).astype(bf16) for i in range(HALF)]
        if n == n_slots:
            ws.append(fill)
        v = jnp.concatenate([jnp.concatenate(vs, axis=1), jnp.concatenate([ones] * len(vs), axis=1)], axis=0)
        weighed.append((dev, peak, v, ws))
    extra = []
    for dev, peak, v, ws in weighed:
        o = jnp.dot(v, jnp.concatenate(ws, axis=0), preferred_element_type=f32)[0:136]
        extra.append((dev, peak, o))

    spot = lax.broadcasted_iota(jnp.int32, (1, rows), 1) // 32
    ready = weigh(scores[0])
    for i in range(HALF):
        peaks, ws = ready
        outs = collect(i, ws)
        if i + 1 < HALF:
            ready = weigh(scores[i + 1])
        wides = []
        for dev, peak, o in extra:
            turn = (dev + (4 - i)) % 4 * 32
            moved = pltpu.roll(peak, turn, 1)
            wides.append(jnp.where(spot == dev, jnp.concatenate([moved] * n_quads, axis=1), NEG))
        top = functools.reduce(jnp.maximum, peaks + wides)
        both = 0.0
        for peak, o in zip(peaks, outs):
            both = both + jnp.exp2((peak - top) * EXPO) * o
        out_ref[i] = both
        for (dev, peak, o), wide in zip(extra, wides):
            turn = (dev + (4 - i)) % 4 * 32
            f = jnp.exp2((wide - top) * EXPO)
            f = sum(f[:, quad * DH : (quad + 1) * DH] for quad in range(n_quads))
            at = pl.ds(pl.multiple_of(dev // 4 * DH, DH), DH)
            out_ref[i, :, at] = out_ref[i, :, at] + pltpu.roll(o, turn, 1) * f
        out_ref[i, 132:136, :] = jnp.broadcast_to(top * EXPO, (4, rows))


def core_merge_kernel(a_ref, b_ref, out_ref):
    rows = a_ref.shape[2]
    high, low = [], []
    for i in range(HALF):
        pa = a_ref[i, 132:133, :]
        pb = b_ref[i, 132:133, :]
        top = jnp.maximum(pa, pb)
        wa = jnp.exp2(pa - top)
        wb = jnp.exp2(pb - top)
        total = a_ref[i, 128:129, :] * wa + b_ref[i, 128:129, :] * wb
        scale = LIFT / total
        o = a_ref[i, 0:128, :] * (wa * scale) + b_ref[i, 0:128, :] * (wb * scale)
        for quad in range(rows // DH):
            out_ref[quad * 4 : quad * 4 + 4, i * 32 : (i + 1) * 32, :] = (
                o[:, quad * DH : (quad + 1) * DH].T.reshape(4, 32, DH)
            )
        lse = top + jnp.log(total) * LOG2E
        far = lse * 8193.0
        head = far - (far - lse)
        high.append(head)
        low.append(lse - head)
    parts = jnp.concatenate(high + low, axis=0)
    for dev in range(rows // 32):
        out_ref[dev, 128:136, :] = parts[:, dev // 4 * DH : (dev // 4 + 1) * DH]


def final_kernel(z_ref, out_ref, w_s, o_s, sems):
    n_dev = z_ref.shape[0]
    pre = lax.axis_index("prefix")
    mine = pl.ds(pl.multiple_of(pre % 4 * 32, 32), 32)
    copies = []
    for c in range(2):
        lses = []
        for src in range(c, n_dev, 2):
            parts = z_ref[src, 128:136, :]
            lses.append(parts[0:4] + parts[4:8])
        top = functools.reduce(jnp.maximum, lses)
        weights = [jnp.exp2(lse - top) for lse in lses]
        scale = 1.0 / (LIFT * sum(weights))
        lines = [w * scale for w in weights]
        lines.append(jnp.zeros((DH - 2 * n_dev, DH), f32))
        w_s[c] = jnp.concatenate(lines, axis=0).T
        columns = w_s[c, mine, :]
        for i in range(HALF):
            o = 0.0
            for y, src in enumerate(range(c, n_dev, 2)):
                o = o + z_ref[src, i * 32 : (i + 1) * 32, :] * columns[:, y * 4 + i : y * 4 + i + 1]
            for g in range(GROUP):
                head = i * GROUP + g
                for s in range(2):
                    r = g * 4 + s * 2
                    o_s[c, s, :, head * DH : (head + 1) * DH] = o[r : r + 2, :].astype(bf16)
        wide = o_s.shape[3]
        copies.append(pltpu.make_async_copy(o_s.at[c], out_ref.at[:, :, c * wide : (c + 1) * wide], sems.at[c]))
        copies[c].start()
    for copy in copies:
        copy.wait()


def call(kernel, out_shape, ins, out_specs=VM, scratch=(), flops=0, moved=0, name=None):
    return pl.pallas_call(
        kernel,
        out_shape=out_shape,
        in_specs=ins,
        out_specs=out_specs,
        scratch_shapes=list(scratch),
        compiler_params=pltpu.CompilerParams(vmem_limit_bytes=40 * 1024 * 1024),
        cost_estimate=pl.CostEstimate(flops=flops, bytes_accessed=moved, transcendentals=0),
        name=name,
    )


def per_device(
    queries,
    prefix_keys,
    prefix_values,
    pool_keys,
    pool_values,
    new_keys,
    new_values,
    block_table,
    suffix_lengths,
):
    n_req = lax.axis_size("req")
    n_pre = lax.axis_size("prefix")
    swap = [(i, i ^ 1) for i in range(n_req)]
    core = [(i, i ^ 1) for i in range(n_pre)]
    across = [(i, (i ^ 1) ^ n_pre) for i in range(n_req * n_pre)]
    pool = jnp.stack([pool_keys, pool_values])
    wide = HALF * DH
    side = lax.axis_index("prefix") % 2
    pool_same = lax.dynamic_slice_in_dim(pool, side * wide, wide, 3)
    pool_cross = lax.dynamic_slice_in_dim(pool, (1 - side) * wide, wide, 3)
    pool_same, pool_cross, queries = lax.optimization_barrier((pool_same, pool_cross, queries))
    far_same = lax.ppermute(pool_same, "req", swap)
    far_cross = lax.ppermute(pool_cross, ("req", "prefix"), across)
    sds = jax.ShapeDtypeStruct
    own = (queries.astype(f32) * QLIFT).astype(jnp.float16)
    own = own.reshape(4, H, DH).transpose(1, 0, 2).reshape(4 * H, DH)
    group = lax.all_gather(own, "prefix", axis=0)
    group = (group.astype(f32) * (1.0 / QLIFT)).astype(bf16)
    rows = n_pre * 32


    def attend(flip, pools):
        return call(
            functools.partial(attend_kernel, flip),
            sds((HALF, 136, rows), f32),
            [VM] * (7 + len(pools)),
            VM,
            [pltpu.SMEM((2 * len(pools), 3), jnp.int32)],
            flops=800_000_000,
            moved=6_000_000,
            name="attend_other" if flip else "attend_own",
        )(
            group, prefix_keys, prefix_values, new_keys, new_values,
            suffix_lengths.reshape(-1, 128), block_table.T, *pools,
        )

    other, far_same, far_cross = lax.optimization_barrier((attend(True, [pool_cross]), far_same, far_cross))
    theirs = lax.ppermute(other, "prefix", core)
    mine = attend(False, [pool_same, far_same, far_cross])
    merged = call(core_merge_kernel, sds((n_pre, 136, DH), f32), [VM, VM], moved=4_000_000, name="core_merge")(
        mine, theirs
    )
    spread = lax.all_to_all(merged.astype(jnp.float16), "prefix", 0, 0, tiled=True)
    return call(
        final_kernel,
        sds((2, 2, H * DH), bf16),
        [VM],
        pl.BlockSpec(memory_space=pl.ANY),
        [
            pltpu.VMEM((2, DH, DH), f32),
            pltpu.VMEM((2, 2, 2, H * DH // 2), bf16),
            pltpu.SemaphoreType.DMA((2,)),
        ],
        moved=1_000_000,
        name="final",
    )(spread.astype(f32))


def solution(mesh):
    placed = (
        P(None, ("req", "prefix"), None),
        P("prefix", None),
        P("prefix", None),
        P(("req", "prefix"), None, None),
        P(("req", "prefix"), None, None),
        P(None, ("req", "prefix"), None),
        P(None, ("req", "prefix"), None),
        P(),
        P(),
    )
    return jax.shard_map(
        per_device,
        mesh=mesh,
        in_specs=placed,
        out_specs=P(None, ("req", "prefix"), None),
        check_vma=False,
    )
```
